128 devices in a mesh: frame: 16 (over z_hi, x, core), tensor: 8 (over y, z_lo).
Axes of the slice: x: 4, y: 4, z: 4 (z_hi: 2, z_lo: 2; z = z_hi * 2 + z_lo), core: 2. Of those that a mesh axis runs over, the one named last changes fastest.
Arguments:
- hidden: bfloat16 [16384, 3072], P(('frame', 'tensor')), may hold values from -24 to 24
- qkv_weight: bfloat16 [3072, 3, 3072], P(None, None, 'tensor'), may hold values from -0.109375 to 0.109375
- norm_gain: float32 [2, 128], replicated, may hold values from 0.5 to 10, as said below
- out_grad: bfloat16 [16384, 3072], P('frame', 'tensor'), may hold values from -0.125 to 0.125
Outputs:
- attended: bfloat16 [16384, 3072], P('frame', 'tensor')
- weight_grad: float32 [3072, 3, 3072], P('frame', None, 'tensor')
The draws below stay inside these ranges and needn't reach their ends.
Inputs may be any that keep to these rules, and one draw needn't show every extreme that they name: `norm_gain`: every gain is positive.
All inputs are finite; a program needn't handle non-finite values.
Results may differ from the reference program's by a relative error of at most 0.028.
The reference program's roundings to bfloat16 on the way (of `weights`, `score_grads` and `qkv_grad`) count: a program that leaves them out, or rounds other values in their place, can miss the bound.
Values may be sent and summed in bfloat16 or wider, within the bound.
No kernel may reach another device: no remote copies, remote signals or barrier semaphores. Data moves between devices by JAX's collectives and lax.ppermute only.
A program may use at most 128 MiB of HBM per device.

```python
import math
import jax
import jax.numpy as jnp
from jax import lax

HEAD_DIM = 128
D = 3072
GROUP = 1024
TOKENS = 16384
N_FRAME = 16


def draw_norm_gain(key, part):
    return jnp.exp(jax.random.uniform(key, (2, HEAD_DIM), jnp.float32, math.log(0.6), math.log(1.8)))


def strengthened(values, stream_key, source, target, parts, factor):
    def block_of(dim):
        return (jnp.arange(values.shape[dim]) // (values.shape[dim] // parts)).reshape((-1,) + (1,) * (values.ndim - 1 - dim))

    first = jax.random.permutation(stream_key, parts)[block_of(target)]
    far = (block_of(target) + parts // 2) % parts
    return jnp.where((block_of(source) == first) | (block_of(source) == far), factor * values, values)


def shard_levels(rng, extent, pieces, least, high):
    def one(position, parts):
        draws = jax.random.uniform(jax.random.fold_in(jax.random.fold_in(rng, 6), position), (parts,), jnp.float32, least / len(pieces), high / len(pieces))
        return jnp.repeat(jnp.exp(draws), extent[position] // parts).reshape((-1,) + (1,) * (len(extent) - position - 1))

    loudness = one(*pieces[0])
    for cut in pieces[1:]:
        loudness = loudness * one(*cut)
    return loudness


def gaussian(stream_key, extent, spread, most, cuts=(), kind=jnp.bfloat16):
    result = spread * jax.random.normal(stream_key, extent, jnp.float32)
    if cuts:
        result = result * shard_levels(stream_key, extent, cuts, -0.22, 0.18)
    return jnp.clip(result, -most, most).astype(kind)


def noise_with(key, shape, scale, limit, pieces, heavy, held_as=jnp.bfloat16):
    drawn = scale * jax.random.normal(key, shape, jnp.float32)
    if pieces:
        drawn = drawn * shard_levels(key, shape, pieces, -0.22, 0.18)
    return jnp.clip(strengthened(drawn, jax.random.fold_in(key, 3), *heavy), -limit, limit).astype(held_as)


def setup_inputs(seed: int = 0) -> dict:
    seeds = jax.random.split(jax.random.key(seed), 5)
    hidden = noise_with(seeds[0], (TOKENS, D), 1.0, 24.0, ((0, 128),), (0, 1, 128, 5.5))
    qkv_weight = gaussian(seeds[1], (D, 3, D), D ** -0.5, 0.109375, ((2, 8),))
    norm_gain = draw_norm_gain(jax.random.fold_in(seeds[4], 71), 0)
    out_grad = gaussian(seeds[3], (TOKENS, D), (TOKENS ** -0.5), 0.125, ((0, 16), (1, 8)))
    return dict(hidden=hidden, qkv_weight=qkv_weight, norm_gain=norm_gain, out_grad=out_grad)


EPSILON = 1e-06

def norm_heads(projected, gain):
    inverse_rms = lax.rsqrt(lax.optimization_barrier(jnp.mean(projected * projected, axis=-1, keepdims=True)) + EPSILON)
    return (projected * inverse_rms * gain, inverse_rms)

def norm_back(projected, inverse_rms, gain, grad):
    weighted = grad * gain
    inner = lax.optimization_barrier(jnp.mean(projected * weighted, axis=-1, keepdims=True))
    return inverse_rms * weighted - projected * (inverse_rms * inverse_rms * inverse_rms) * inner

def product(form, left, right):
    return jnp.einsum(form, left.astype(jnp.float32), right.astype(jnp.float32))

def window_attention(query, window, out_grad, valid):
    total_rows = query.shape[0]
    block = min(512, total_rows)
    keys = window[:, 0]
    values = window[:, 1]
    factor = query.shape[-1] ** (-0.5)
    output_list = []
    query_grads = []
    keyval_grad = jnp.zeros(window.shape, jnp.float32)
    for first_row in range(0, total_rows, block):
        query_block = query[first_row:first_row + block]
        grad_block = out_grad[first_row:first_row + block]
        scores = product('qhd,khd->hqk', query_block, keys) * factor
        scores = jnp.where(valid[None, None, :], scores, -1e+30)
        peak = lax.optimization_barrier(jnp.max(scores, axis=-1, keepdims=True))
        raised = jnp.exp(scores - peak)
        weights = (raised / lax.optimization_barrier(jnp.sum(raised, axis=-1, keepdims=True))).astype(jnp.bfloat16)
        attended = product('hqk,khd->qhd', weights, values).astype(jnp.bfloat16)
        row_dots = lax.optimization_barrier(jnp.sum(grad_block.astype(jnp.float32) * attended.astype(jnp.float32), axis=-1))
        prob_grads = product('qhd,khd->hqk', grad_block, values)
        score_grads = (weights.astype(jnp.float32) * (prob_grads - row_dots.T[:, :, None])).astype(jnp.bfloat16)
        query_grad = product('hqk,khd->qhd', score_grads, keys) * factor
        key_grad = product('hqk,qhd->khd', score_grads, query_block) * factor
        value_grad = product('hqk,qhd->khd', weights, grad_block)
        keyval_grad = keyval_grad + jnp.stack([key_grad, value_grad], axis=1)
        output_list.append(attended)
        query_grads.append(query_grad)
    return (jnp.concatenate(output_list, 0), jnp.concatenate(query_grads, 0), keyval_grad)

def reference(hidden, qkv_weight, norm_gain, out_grad):
    tokens, width = hidden.shape
    heads = width // HEAD_DIM
    projected = jnp.dot(hidden, qkv_weight.reshape(width, 3 * width), preferred_element_type=jnp.float32)
    projected = projected.reshape(tokens, 3, heads, HEAD_DIM)
    query_normed, query_rms = norm_heads(projected[:, 0], norm_gain[0])
    key_normed, key_rms = norm_heads(projected[:, 1], norm_gain[1])
    query = query_normed.astype(jnp.bfloat16)
    keyval = jnp.stack([key_normed.astype(jnp.bfloat16), projected[:, 2].astype(jnp.bfloat16)], 1)
    half = GROUP // 2
    padded = jnp.pad(keyval, ((half, half), (0, 0), (0, 0), (0, 0)))
    grads_heads = out_grad.reshape(tokens, heads, HEAD_DIM)

    def one_group(group_index):
        start = (group_index * GROUP).astype(jnp.int32)
        window = lax.dynamic_slice_in_dim(padded, start, 2 * GROUP, 0)
        query_rows = lax.dynamic_slice_in_dim(query, start, GROUP, 0)
        grad_rows = lax.dynamic_slice_in_dim(grads_heads, start, GROUP, 0)
        place = start + jnp.arange(2 * GROUP, dtype=jnp.int32)
        valid = (place >= half) & (place < tokens + half)
        return window_attention(query_rows, window, grad_rows, valid)
    outputs, query_grads, keyval_grads = lax.map(one_group, jnp.arange(N_FRAME, dtype=jnp.int32))
    lower = keyval_grads[:, :half]
    own = keyval_grads[:, half:half + GROUP]
    upper = keyval_grads[:, half + GROUP:]
    zero_rows = jnp.zeros_like(lower[:1])
    from_prev = jnp.concatenate([zero_rows, upper[:-1]], 0)
    from_next = jnp.concatenate([lower[1:], zero_rows], 0)
    keyval_grad = (own + jnp.concatenate([from_prev, from_next], 1)).reshape(tokens, 2, heads, HEAD_DIM)
    query_grad = query_grads.reshape(tokens, heads, HEAD_DIM)
    query_raw_grad = norm_back(projected[:, 0], query_rms, norm_gain[0], query_grad)
    key_raw_grad = norm_back(projected[:, 1], key_rms, norm_gain[1], keyval_grad[:, 0])
    qkv_grad = jnp.stack([query_raw_grad, key_raw_grad, keyval_grad[:, 1]], 1).astype(jnp.bfloat16)
    qkv_grad = qkv_grad.reshape(tokens, 3 * width)
    weight_grad = jnp.dot(hidden.T, qkv_grad, preferred_element_type=jnp.float32).reshape(width, 3, width)
    return (outputs.reshape(tokens, width), weight_grad)
```

```python
import functools

import jax
import jax.numpy as jnp
from jax import lax
from jax.experimental import pallas as pl
from jax.experimental.pallas import tpu as pltpu
from jax.sharding import PartitionSpec as P

HEAD_DIM = 128
EPSILON = 1e-06
LOG2E = 1.4426950408889634
F32 = jnp.float32
BF16 = jnp.bfloat16
NN = (((1,), (0,)), ((), ()))
NT = (((1,), (1,)), ((), ()))
PARAMS = pltpu.CompilerParams(vmem_limit_bytes=56 * 1024 * 1024)


def dot(left, right, dims=NN):
    return lax.dot_general(left, right, dims, preferred_element_type=F32)


def whole(*shape):
    return pl.BlockSpec(shape, lambda *_: (0,) * len(shape))


def frame_pairs(dx, dz, dc=0):
    return [
        (zh * 8 + x * 2 + c, ((zh + dz) % 2) * 8 + ((x + dx) % 4) * 2 + (c + dc) % 2)
        for zh in range(2)
        for x in range(4)
        for c in range(2)
    ]


def tensor_pairs(dy, dz):
    return [
        (y * 2 + z, ((y + dy) % 4) * 2 + (z + dz) % 2) for y in range(4) for z in range(2)
    ]


def proj_kernel(heads, index_ref, x_ref, w_ref, gain_ref, *refs):
    q_ref, kv_ref, raw_ref, turned_ref = refs[-4:]
    x = x_ref[...]
    turned_ref[...] = x.T
    for kind in range(3):
        width = heads * HEAD_DIM
        projected = dot(x, w_ref[:, kind * width : (kind + 1) * width])
        for h in range(heads):
            part = projected[:, h * HEAD_DIM : (h + 1) * HEAD_DIM]
            if kind == 2:
                kv_ref[heads + h] = part.astype(BF16)
                continue
            raw_ref[kind * heads + h] = part
            inverse_rms = lax.rsqrt(jnp.mean(part * part, axis=-1, keepdims=True) + EPSILON)
            normed = (part * inverse_rms * gain_ref[kind : kind + 1]).astype(BF16)
            if kind == 0:
                q_ref[h] = normed
            else:
                kv_ref[h] = normed


def project(index, chunks, weight, gain, heads, total, before=None):
    count, rows, depth = chunks.shape
    shapes = [
        jax.ShapeDtypeStruct((heads, total, HEAD_DIM), BF16),
        jax.ShapeDtypeStruct((2 * heads, total, HEAD_DIM), BF16),
        jax.ShapeDtypeStruct((2 * heads, total, HEAD_DIM), F32),
        jax.ShapeDtypeStruct((depth, total), BF16),
    ]
    out_specs = [
        pl.BlockSpec((s.shape[0], rows, HEAD_DIM), lambda i, index: (0, index[i], 0))
        for s in shapes[:3]
    ] + [pl.BlockSpec((depth, rows), lambda i, index: (0, index[i]))]
    in_specs = [
        pl.BlockSpec((None, rows, depth), lambda i, index: (i, 0, 0)),
        whole(*weight.shape),
        whole(*gain.shape),
    ]
    aliases = {}
    args = [index, chunks, weight, gain]
    if before is not None:
        in_specs += [pl.BlockSpec(memory_space=pl.ANY)] * 4
        aliases = {4 + i: i for i in range(4)}
        args += list(before)
    return pl.pallas_call(
        functools.partial(proj_kernel, heads),
        grid_spec=pltpu.PrefetchScalarGridSpec(
            num_scalar_prefetch=1, grid=(count,), in_specs=in_specs, out_specs=out_specs
        ),
        out_shape=shapes,
        input_output_aliases=aliases,
        compiler_params=PARAMS,
        name="project",
    )(*args)


def attention_kernel(
    block, span, bias_ref, q_ref, own_k, own_v, far_k, far_v, grad_ref, raw_ref, gain_ref,
    out_ref, gq_ref, dk_ref, dv_ref, low_ref, high_ref, dk_sum, dv_sum,
):
    rows = q_ref.shape[0]
    half = rows // 2
    factor = HEAD_DIM**-0.5
    scale = factor * LOG2E
    step = pl.program_id(0)
    own = rows // span

    def part(own_ref, far_ref, j):
        if j < own:
            return own_ref[j * span : (j + 1) * span]
        return far_ref[(j - own) * span : (j - own + 1) * span]

    here = pl.ds(pl.multiple_of(step * block, block), block)
    query = q_ref[here]
    grad = grad_ref[here]
    scores = []
    for j in range(2 * own):
        one = dot(query, part(own_k, far_k, j), NT)
        if j >= own:
            one = one + bias_ref[0 if (j - own) * span < half else 1]
        scores.append(one)
    peak = functools.reduce(jnp.maximum, [jnp.max(s, axis=-1, keepdims=True) for s in scores])
    peak = peak * scale
    total = 0.0
    mixed = 0.0
    weights = []
    for j in range(2 * own):
        raised = jnp.exp2(scores[j] * scale - peak)
        total = total + jnp.sum(raised, axis=-1, keepdims=True)
        raised = raised.astype(BF16)
        weights.append(raised)
        mixed = mixed + dot(raised, part(own_v, far_v, j))
    inverse = 1.0 / total
    attended = (mixed * inverse).astype(BF16)
    out_ref[here] = attended
    grad_wide = grad.astype(F32)
    row_dots = jnp.sum(grad_wide * attended.astype(F32), axis=-1, keepdims=True)
    query_turned = (query.astype(F32) * inverse).astype(BF16).T
    grad_turned = (grad_wide * inverse).astype(BF16).T
    query_grad = 0.0
    for j in range(2 * own):
        columns = slice(j * span, (j + 1) * span)
        prob_grads = dot(grad, part(own_v, far_v, j), NT)
        score_grads = (weights[j].astype(F32) * (prob_grads - row_dots)).astype(BF16)
        query_grad = query_grad + dot(score_grads, part(own_k, far_k, j))
        key_part = dot(query_turned, score_grads)
        value_part = dot(grad_turned, weights[j])

        @pl.when(step == 0)
        def _():
            dk_sum[:, columns] = key_part
            dv_sum[:, columns] = value_part

        @pl.when(step > 0)
        def _():
            dk_sum[:, columns] += key_part
            dv_sum[:, columns] += value_part

    gq_ref[here] = norm_back(raw_ref[here], gain_ref[0:1], query_grad * (inverse * factor))

    @pl.when(step == pl.num_programs(0) - 1)
    def _():
        dk_ref[...] = dk_sum[:, :rows].T * factor
        dv_ref[...] = dv_sum[:, :rows].T
        low_ref[0] = (dk_sum[:, rows : rows + half].T * factor).astype(BF16)
        low_ref[1] = dv_sum[:, rows : rows + half].T.astype(BF16)
        high_ref[0] = (dk_sum[:, rows + half :].T * factor).astype(BF16)
        high_ref[1] = dv_sum[:, rows + half :].T.astype(BF16)


def norm_back(raw, gain, grad):
    inverse_rms = lax.rsqrt(jnp.mean(raw * raw, axis=-1, keepdims=True) + EPSILON)
    weighted = grad * gain
    unit = raw * inverse_rms
    inner = jnp.mean(unit * weighted, axis=-1, keepdims=True)
    return (inverse_rms * (weighted - unit * inner)).astype(BF16)


def attention(bias, q, kv, far, out_grad, raw, gain, h, block=512, span=512):
    heads, rows, _ = q.shape
    half = rows // 2
    pick = lambda a: pl.BlockSpec((None, rows, HEAD_DIM), lambda i: (a, 0, 0))
    bf16 = lambda *s: jax.ShapeDtypeStruct(s, BF16)
    f32 = lambda *s: jax.ShapeDtypeStruct(s, F32)
    return pl.pallas_call(
        functools.partial(attention_kernel, block, span),
        grid=(rows // block,),
        in_specs=[
            pl.BlockSpec(memory_space=pltpu.SMEM),
            pick(h),
            pick(h),
            pick(heads + h),
            pick(h),
            pick(heads + h),
            pl.BlockSpec((rows, HEAD_DIM), lambda i: (0, h)),
            pick(h),
            whole(*gain.shape),
        ],
        out_specs=[whole(rows, HEAD_DIM)] * 4 + [whole(2, half, HEAD_DIM)] * 2,
        out_shape=[bf16(rows, HEAD_DIM)] * 2 + [f32(rows, HEAD_DIM)] * 2
        + [bf16(2, half, HEAD_DIM)] * 2,
        scratch_shapes=[pltpu.VMEM((HEAD_DIM, 2 * rows), F32)] * 2,
        compiler_params=PARAMS,
        name="attention",
    )(bias, q, kv, kv, far, far, out_grad, raw, gain)


def other_kernel(
    place_ref, turned_ref, gq_ref, dk_ref, dv_ref, prev_ref, next_ref, raw_ref, gain_ref,
    out_ref, g_ref,
):
    half = gq_ref.shape[0] // 2

    @pl.when(pl.program_id(0) == 0)
    def _():
        g_ref[:, :HEAD_DIM] = gq_ref[...]
        for i, came in enumerate((prev_ref, next_ref)):
            rows = slice(i * half, (i + 1) * half)
            dk = dk_ref[rows] + came[0].astype(F32)
            dv = dv_ref[rows] + came[1].astype(F32)
            g_ref[rows, HEAD_DIM : 2 * HEAD_DIM] = norm_back(raw_ref[rows], gain_ref[1:2], dk)
            g_ref[rows, 2 * HEAD_DIM :] = dv.astype(BF16)

    blocks, rows, depth = turned_ref.shape
    product = dot(turned_ref[...].reshape(blocks * rows, depth), g_ref[...])
    out_ref[...] = product.astype(BF16).reshape(out_ref.shape)


def other_rows(place, turned, gq, dk, dv, prev, following, raw, gain, h):
    groups, _, rows, depth = turned.shape
    heads = raw.shape[0] // 2
    take = 2
    width = 3 * HEAD_DIM
    return pl.pallas_call(
        other_kernel,
        grid_spec=pltpu.PrefetchScalarGridSpec(
            num_scalar_prefetch=1,
            grid=(groups // take,),
            in_specs=[
                pl.BlockSpec((take, None, rows, depth), lambda i, p: (i, 1 - p[2], 0, 0)),
                whole(*gq.shape),
                whole(*dk.shape),
                whole(*dv.shape),
                whole(*prev.shape),
                whole(*following.shape),
                pl.BlockSpec((None, depth, HEAD_DIM), lambda i, p: (heads + h, 0, 0)),
                whole(*gain.shape),
            ],
            out_specs=[
                pl.BlockSpec((take, rows, width), lambda i, p: (i, 0, 0)),
                whole(depth, width),
            ],
        ),
        out_shape=[
            jax.ShapeDtypeStruct((groups, rows, width), BF16),
            jax.ShapeDtypeStruct((depth, width), BF16),
        ],
        compiler_params=PARAMS,
        name="other_rows",
    )(place, turned, gq, dk, dv, prev, following, raw, gain)


def own_kernel(place_ref, turned_ref, g_ref, came_ref, *refs):
    outs, held = refs[:-1], refs[-1]
    step = pl.program_id(0)
    blocks, rows, depth = turned_ref.shape
    product = dot(turned_ref[...].reshape(blocks * rows, depth), g_ref[...])
    for b in range(blocks):
        one = product[b * rows : (b + 1) * rows] + came_ref[b].astype(F32)
        held[step * blocks + b] = one.astype(BF16)

    @pl.when(step == pl.num_programs(0) - 1)
    def _():
        zh, x = place_ref[0], place_ref[1]
        for dx in range(4):
            for dz in range(2):
                outs[dx][dz] = held[((zh + dz) % 2) * 4 + (x + dx) % 4]


def own_rows(place, turned, g, came):
    groups, _, rows, depth = turned.shape
    take = 2
    width = g.shape[1]
    return pl.pallas_call(
        own_kernel,
        grid_spec=pltpu.PrefetchScalarGridSpec(
            num_scalar_prefetch=1,
            grid=(groups // take,),
            in_specs=[
                pl.BlockSpec((take, None, rows, depth), lambda i, p: (i, p[2], 0, 0)),
                whole(depth, width),
                pl.BlockSpec((take, rows, width), lambda i, p: (i, 0, 0)),
            ],
            out_specs=[whole(2, rows, width)] * 4,
            scratch_shapes=[pltpu.VMEM((groups, rows, width), BF16)],
        ),
        out_shape=[jax.ShapeDtypeStruct((2, rows, width), BF16)] * 4,
        compiler_params=PARAMS,
        name="own_rows",
    )(place, turned, g, came)


def per_device(hidden, qkv_weight, norm_gain, out_grad):
    depth, kinds, local = qkv_weight.shape
    heads = local // HEAD_DIM
    chunk = hidden.shape[0]
    total = chunk * lax.axis_size("tensor")
    half = total // 2
    frame = lax.axis_index("frame").astype(jnp.int32)
    frames = lax.axis_size("frame")
    tensor = lax.axis_index("tensor").astype(jnp.int32)
    zh, x, core = frame // 8, (frame // 2) % 4, frame % 2
    y, zl = tensor // 2, tensor % 2
    place = jnp.stack([zh, x, core])

    def at(dy, dz):
        return ((y + dy) % 4) * 2 + (zl + dz) % 2

    weight = qkv_weight.reshape(depth, kinds * local)

    send = lambda value, dy, dz: lax.ppermute(value, "tensor", tensor_pairs(dy, dz))
    cut = chunk // 2
    below = send(hidden, 1, 0)
    above = send(hidden, -1, 0)
    side = send(hidden, 0, 1)
    far_a = send(below[:cut], 1, 0)
    far_b = send(above[cut:], -1, 0)
    side_above_a = send(above[:cut], 0, 1)
    side_above_b = send(above[cut:], 0, 1)
    side_below = send(side, 1, 0)
    side_far_a = send(side_above_a, -1, 0)
    side_far_b = send(far_b, 0, 1)

    index = jnp.stack([at(0, 0), at(-1, 0), at(1, 0), at(0, 1)])
    state = project(
        index, jnp.stack([hidden, below, above, side]), weight, norm_gain, heads, total
    )
    index = jnp.stack([at(2, 0), at(-1, 1), at(1, 1)])
    chunks = jnp.concatenate([far_a, far_b, side_below, side_above_a, side_above_b])
    state = project(
        index, chunks.reshape(3, chunk, depth), weight, norm_gain, heads, total, state
    )
    index = at(2, 1)[None]
    chunks = jnp.concatenate([side_far_a, side_far_b])
    state = project(
        index, chunks.reshape(1, chunk, depth), weight, norm_gain, heads, total, state
    )
    q, kv, raw, turned = state
    turned = turned.reshape(8, 2, depth // 16, total)

    up = [(i, i + 1) for i in range(frames - 1)]
    down = [(j, i) for i, j in up]
    from_next = lax.ppermute(kv[:, :half], "frame", down)
    from_prev = lax.ppermute(kv[:, half:], "frame", up)
    far = jnp.concatenate([from_next, from_prev], 1)
    bias = jnp.stack(
        [
            jnp.where(frame < frames - 1, 0.0, -1e30).astype(F32),
            jnp.where(frame > 0, 0.0, -1e30).astype(F32),
        ]
    )

    outs = []
    sums = []
    for h in range(heads):
        attended, gq, dk, dv, low, high = attention(
            bias, q, kv, far, out_grad, raw, norm_gain, h
        )
        outs.append(attended)
        came_prev = lax.ppermute(low, "frame", up)
        came_next = lax.ppermute(high, "frame", down)
        theirs, g = other_rows(
            place, turned, gq, dk, dv, came_prev, came_next, raw, norm_gain, h
        )
        came = lax.ppermute(theirs, "frame", frame_pairs(0, 0, 1))
        pieces = own_rows(place, turned, g, came)
        summed = pieces[0].astype(F32)
        for dx in (1, 3, 2):
            summed = summed + lax.ppermute(pieces[dx], "frame", frame_pairs(dx, 0)).astype(F32)
        other = lax.ppermute(summed[1].astype(BF16), "frame", frame_pairs(0, 1))
        sums.append(summed[0] + other.astype(F32))
    weight_grad = jnp.stack([s.reshape(-1, 3, HEAD_DIM) for s in sums], 2)
    return (jnp.concatenate(outs, 1), weight_grad.reshape(-1, 3, local))


def solution(mesh):
    placed = (P(("frame", "tensor"), None), P(None, None, "tensor"), P(), P("frame", "tensor"))
    return jax.shard_map(
        per_device,
        mesh=mesh,
        in_specs=placed,
        out_specs=(P("frame", "tensor"), P("frame", None, "tensor")),
        check_vma=False,
    )
```

```python
import functools

import jax
import jax.numpy as jnp
from jax import lax
from jax.experimental import pallas as pl
from jax.experimental.pallas import tpu as pltpu
from jax.sharding import PartitionSpec as P

HEAD_DIM = 128
EPSILON = 1e-06
LOG2E = 1.4426950408889634
LIMIT = 16
FIRST = 4
F32 = jnp.float32
BF16 = jnp.bfloat16
NN = (((1,), (0,)), ((), ()))
NT = (((1,), (1,)), ((), ()))
TN = (((0,), (0,)), ((), ()))


def dot(left, right, dims=NN):
    return lax.dot_general(left, right, dims, preferred_element_type=F32)


def on_chip(kernel, ins, outs, scratch=(), limit=LIMIT, aliases=None, us=1, name=None):
    specs, args = [], []
    for one in ins:
        space = pltpu.VMEM
        if isinstance(one, tuple):
            one, space = one
        specs.append(pl.BlockSpec(memory_space=space))
        args.append(one)
    return pl.pallas_call(
        kernel,
        in_specs=specs,
        out_specs=[pl.BlockSpec(memory_space=pltpu.VMEM)] * len(outs),
        out_shape=[jax.ShapeDtypeStruct(shape, dtype) for shape, dtype in outs],
        scratch_shapes=list(scratch),
        input_output_aliases=aliases or {},
        compiler_params=pltpu.CompilerParams(vmem_limit_bytes=limit * 1024 * 1024),
        cost_estimate=pl.CostEstimate(
            flops=int(us * 1.1e9), bytes_accessed=0, transcendentals=0
        ),
        name=name,
    )(*args)


def frame_pairs(dx, dz, dc=0):
    return [
        (zh * 8 + x * 2 + c, ((zh + dz) % 2) * 8 + ((x + dx) % 4) * 2 + (c + dc) % 2)
        for zh in range(2)
        for x in range(4)
        for c in range(2)
    ]


def tensor_pairs(dy, dz):
    return [
        (y * 2 + z, ((y + dy) % 4) * 2 + (z + dz) % 2) for y in range(4) for z in range(2)
    ]


def half_pairs(sign):
    pairs = []
    for f in range(16):
        for t in range(8):
            there = f + (sign if t // 4 else -sign)
            if 0 <= there < 16:
                pairs.append((f * 8 + t, there * 8 + t))
    return pairs


def proj_kernel(heads, groups, first, extra, place_ref, gain_ref, w_ref, *refs):
    outs = refs[len(refs) - 4 - extra :]
    q_ref, kv_ref, raw_ref, all_ref = outs[:4]
    chunks = []
    at = 0
    for count in groups:
        chunks.append(jnp.concatenate([r[...] for r in refs[at : at + count]], 0))
        at += count
    rows = chunks[0].shape[0]
    x = jnp.concatenate(chunks, 0)
    begin = (first - FIRST) * rows
    all_ref[begin : begin + x.shape[0]] = x
    for kind in (1, 2, 0):
        projected = dot(x, w_ref[kind])
        for h in range(heads):
            part = projected[:, h * HEAD_DIM : (h + 1) * HEAD_DIM]
            if kind < 2:
                inverse_rms = lax.rsqrt(jnp.mean(part * part, axis=-1, keepdims=True) + EPSILON)
                normed = (part * inverse_rms * gain_ref[kind : kind + 1]).astype(BF16)
            else:
                normed = part.astype(BF16)
            for i in range(len(groups)):
                there = pl.ds(pl.multiple_of(place_ref[first + i] * rows, rows), rows)
                here = slice(i * rows, (i + 1) * rows)
                if kind < 2:
                    raw_ref[kind * heads + h, there] = part[here]
                if kind == 0:
                    q_ref[h, there] = normed[here]
                else:
                    kv_ref[(kind - 1) * heads + h, there] = normed[here]
                if kind > 0 and extra == 1:
                    outs[4][(kind - 1) * heads + h] = normed
    if extra == 2:
        half = kv_ref.shape[1] // 2
        for i, out in enumerate(outs[4:]):
            mine = place_ref[3] if i == 0 else 1 - place_ref[3]
            out[...] = kv_ref[:, pl.ds(pl.multiple_of(mine * half, half), half)]


def project(place, first, groups, weight, gain, heads, total, before, extra, us):
    rows = sum(piece.shape[0] for piece in groups[0])
    outs = [
        ((heads, total, HEAD_DIM), BF16),
        ((2 * heads, total, HEAD_DIM), BF16),
        ((2 * heads, total, HEAD_DIM), F32),
        ((total, weight.shape[1]), BF16),
    ]
    outs += [((2 * heads, total // 2 if extra == 2 else rows, HEAD_DIM), BF16)] * extra
    ins = [(place, pltpu.SMEM), gain, weight] + [piece for group in groups for piece in group]
    aliases = {}
    if before is not None:
        aliases = {len(ins) + i: i for i in range(4)}
        ins += list(before)
    counts = tuple(len(group) for group in groups)
    return on_chip(
        functools.partial(proj_kernel, heads, counts, FIRST + first, extra),
        ins,
        outs,
        aliases=aliases,
        us=us,
        name="project",
    )


def attention_kernel(
    h, block, span, bias_ref, place_ref, q_ref, kv_ref, same_ref, cross_ref, patch_ref, grad_ref,
    raw_ref, gain_ref, after_ref,
    out_ref, gq_ref, dk_ref, dv_ref, low_ref, high_ref, keys, values, dk_sum, dv_sum,
):
    heads, rows, _ = q_ref.shape
    half = rows // 2
    factor = HEAD_DIM**-0.5
    scale = factor * LOG2E
    chunk = patch_ref.shape[1]
    there = rows + half + (place_ref[FIRST + rows // chunk - 1] % (half // chunk)) * chunk
    there = pl.ds(pl.multiple_of(there, chunk), chunk)
    for wide, i in ((keys, h), (values, heads + h)):
        wide[:rows, :HEAD_DIM] = kv_ref[i]
        wide[rows : rows + half, :HEAD_DIM] = same_ref[i]
        wide[rows + half :, :HEAD_DIM] = cross_ref[i]
        wide[there, :HEAD_DIM] = patch_ref[i]
    lane = lax.broadcasted_iota(jnp.int32, (2 * rows, HEAD_DIM), 1)
    values[:, HEAD_DIM:] = jnp.where(lane < 3, -1.0, 0.0).astype(BF16)
    keys[:rows, HEAD_DIM:] = jnp.zeros((rows, HEAD_DIM), BF16)
    for i in range(2):
        first = rows + i * half
        keys[first : first + half, HEAD_DIM:] = jnp.where(
            lane[:half] == 0, bias_ref[i], 0.0
        ).astype(BF16)
    lane = lane[:block]
    one = jnp.where(lane == 0, 1.0, 0.0).astype(BF16)
    for step in range(rows // block):
        here = slice(step * block, (step + 1) * block)
        query = q_ref[h, here]
        grad = grad_ref[here, h * HEAD_DIM : (h + 1) * HEAD_DIM]
        parts = [slice(j * span, (j + 1) * span) for j in range(2 * rows // span)]
        query_wide = jnp.concatenate([query, one], 1)
        scores = [dot(query_wide, keys[p], NT) for p in parts]
        peak = functools.reduce(jnp.maximum, [jnp.max(s, axis=-1, keepdims=True) for s in scores])
        peak = peak * scale
        mixed = 0.0
        weights = []
        for p, one_scores in zip(parts, scores):
            raised = jnp.exp2(one_scores * scale - peak).astype(BF16)
            weights.append(raised)
            mixed = mixed + dot(raised, values[p])
        inverse = -1.0 / mixed[:, HEAD_DIM : HEAD_DIM + 1]
        attended = (mixed[:, :HEAD_DIM] * inverse).astype(BF16)
        out_ref[here] = attended
        grad_f32 = grad.astype(F32)
        dots = jnp.sum(grad_f32 * attended.astype(F32), axis=-1, keepdims=True)
        dots_a = dots.astype(BF16)
        dots = dots - dots_a.astype(F32)
        dots_b = dots.astype(BF16)
        dots_c = (dots - dots_b.astype(F32)).astype(BF16)
        zero = jnp.zeros_like(dots_c)
        tail = jnp.where(
            lane == 0, dots_a, jnp.where(lane == 1, dots_b, jnp.where(lane == 2, dots_c, zero))
        )
        grad_wide = jnp.concatenate([grad, tail], 1)
        query_turned = (query.astype(F32) * inverse).astype(BF16).T
        grad_turned = (grad_f32 * inverse).astype(BF16).T
        query_grad = 0.0
        for p, one_weights in zip(parts, weights):
            prob_grads = dot(grad_wide, values[p], NT)
            score_grads = (one_weights.astype(F32) * prob_grads).astype(BF16)
            query_grad = query_grad + dot(score_grads, keys[p, :HEAD_DIM])
            key_part = dot(query_turned, score_grads)
            value_part = dot(grad_turned, one_weights)
            if step == 0:
                dk_sum[:, p] = key_part
                dv_sum[:, p] = value_part
            else:
                dk_sum[:, p] += key_part
                dv_sum[:, p] += value_part
        gq_ref[here] = norm_back(raw_ref[h, here], gain_ref[0:1], query_grad * (inverse * factor))
    dk_ref[...] = dk_sum[:, :rows].T * factor
    dv_ref[...] = dv_sum[:, :rows].T
    low_ref[0] = (dk_sum[:, rows : rows + half].T * factor).astype(BF16)
    low_ref[1] = dv_sum[:, rows : rows + half].T.astype(BF16)
    high_ref[0] = (dk_sum[:, rows + half :].T * factor).astype(BF16)
    high_ref[1] = dv_sum[:, rows + half :].T.astype(BF16)


def norm_back(raw, gain, grad):
    inverse_rms = lax.rsqrt(jnp.mean(raw * raw, axis=-1, keepdims=True) + EPSILON)
    weighted = grad * gain
    unit = raw * inverse_rms
    inner = jnp.mean(unit * weighted, axis=-1, keepdims=True)
    return (inverse_rms * (weighted - unit * inner)).astype(BF16)


def attention(bias, place, q, kv, far, out_grad, raw, gain, h, after, block=512, span=512):
    heads, rows, _ = q.shape
    half = rows // 2
    return on_chip(
        functools.partial(attention_kernel, h, block, span),
        [(bias, pltpu.SMEM), (place, pltpu.SMEM), q, kv, *far, out_grad, raw, gain, (after, pl.ANY)],
        [((rows, HEAD_DIM), BF16)] * 2
        + [((rows, HEAD_DIM), F32)] * 2
        + [((2, half, HEAD_DIM), BF16)] * 2,
        [pltpu.VMEM((2 * rows, 2 * HEAD_DIM), BF16)] * 2 + [pltpu.VMEM((HEAD_DIM, 2 * rows), F32)] * 2,
        us=11,
        name="attention",
    )


def grad_kernel(
    h, count, place_ref, gq_ref, dk_ref, dv_ref, same_ref, cross_ref, raw_ref, gain_ref, after_ref,
    all_ref, mine_ref, theirs_ref, straight, g,
):
    total = gq_ref.shape[0]
    half = total // 2
    chunk = total // count
    straight[:, :HEAD_DIM] = gq_ref[...]
    for i, came in enumerate((same_ref, cross_ref)):
        mine = place_ref[3] if i == 0 else 1 - place_ref[3]
        rows = pl.ds(pl.multiple_of(mine * half, half), half)
        dk = dk_ref[rows] + came[0].astype(F32)
        dv = dv_ref[rows] + came[1].astype(F32)
        straight[rows, HEAD_DIM : 2 * HEAD_DIM] = norm_back(
            raw_ref[raw_ref.shape[0] // 2 + h, rows], gain_ref[1:2], dk
        )
        straight[rows, 2 * HEAD_DIM :] = dv.astype(BF16)
    for i in range(count):
        there = pl.ds(pl.multiple_of(place_ref[FIRST + i] * chunk, chunk), chunk)
        g[i * chunk : (i + 1) * chunk] = straight[there]
    blocks, rows, _ = mine_ref.shape
    low = place_ref[2] == 0
    for b in range(blocks):
        columns = slice(2 * b * rows, 2 * (b + 1) * rows)
        product = dot(all_ref[:, columns], g[...], TN).astype(BF16)
        mine_ref[b] = jnp.where(low, product[:rows], product[rows:])
        theirs_ref[b] = jnp.where(low, product[rows:], product[:rows])


def weight_rows(h, place, count, gathered, gq, dk, dv, same, cross, raw, gain, after):
    total = gq.shape[0]
    width = 3 * HEAD_DIM
    out = ((8, gathered.shape[1] // 16, width), BF16)
    return on_chip(
        functools.partial(grad_kernel, h, count),
        [(place, pltpu.SMEM), gq, dk, dv, same, cross, raw, gain, (after, pl.ANY), gathered],
        [out, out],
        [pltpu.VMEM((total, width), BF16)] * 2,
        us=6,
        name="weight_rows",
    )


def pair_kernel(place_ref, mine_ref, came_ref, *outs):
    zh, x = place_ref[0], place_ref[1]
    for dx in range(4):
        for dz in range(2):
            b = ((zh + dz) % 2) * 4 + (x + dx) % 4
            outs[dx][dz] = (mine_ref[b].astype(F32) + came_ref[b].astype(F32)).astype(BF16)


def pair_sum(place, mine, came):
    return on_chip(
        pair_kernel, [(place, pltpu.SMEM), mine, came], [((2,) + mine.shape[1:], BF16)] * 4, name="pair"
    )


def line_kernel(a_ref, b_ref, c_ref, d_ref, keep_ref, send_ref):
    for i, out in enumerate((keep_ref, send_ref)):
        summed = a_ref[i].astype(F32) + b_ref[i].astype(F32)
        summed = summed + c_ref[i].astype(F32) + d_ref[i].astype(F32)
        out[...] = summed.astype(out.dtype)


def last_kernel(heads, *refs):
    out = refs[-1]
    for h in range(heads):
        total = refs[h][...] + refs[heads + h][...].astype(F32)
        for kind in range(3):
            out[kind, :, h * HEAD_DIM : (h + 1) * HEAD_DIM] = total[
                :, kind * HEAD_DIM : (kind + 1) * HEAD_DIM
            ]


def halves_kernel(below_ref, above_ref, below_a, above_a, above_b):
    cut = below_a.shape[0]
    below_a[...] = below_ref[:cut]
    above_a[...] = above_ref[:cut]
    above_b[...] = above_ref[cut:]


def per_device(hidden, qkv_weight, norm_gain, out_grad):
    depth, kinds, local = qkv_weight.shape
    heads = local // HEAD_DIM
    chunk = hidden.shape[0]
    total = chunk * lax.axis_size("tensor")
    half = total // 2
    frame = lax.axis_index("frame").astype(jnp.int32)
    frames = lax.axis_size("frame")
    tensor = lax.axis_index("tensor").astype(jnp.int32)
    zh, x, core = frame // 8, (frame // 2) % 4, frame % 2
    y, zl = tensor // 2, tensor % 2
    def at(dy, dz):
        return ((y + dy) % 4) * 2 + (zl + dz) % 2

    weight = qkv_weight.transpose(1, 0, 2)

    send = lambda value, dy, dz: lax.ppermute(value, "tensor", tensor_pairs(dy, dz))
    cut = chunk // 2
    below = send(hidden, 1, 0)
    above = send(hidden, -1, 0)
    side = send(hidden, 0, 1)
    below_a, above_a, above_b = on_chip(
        halves_kernel, [below, above], [((cut, depth), BF16)] * 3, name="halves"
    )
    far_a = send(below_a, 1, 0)
    side_above_a = send(above_a, 0, 1)
    far_b = send(above_b, -1, 0)
    side_above_b = send(above_b, 0, 1)
    side_below = send(side, 1, 0)
    side_far_a = send(side_above_a, -1, 0)
    side_far_b = send(far_b, 0, 1)
    groups = [
        (hidden,),
        (below,),
        (above,),
        (side,),
        (far_a, far_b),
        (side_below,),
        (side_above_a, side_above_b),
        (side_far_a, side_far_b),
    ]
    moves = [(0, 0), (-1, 0), (1, 0), (0, 1), (2, 0), (-1, 1), (1, 1), (2, 1)]
    mine = y // 2
    place = jnp.stack([zh, x, core, mine] + [at(*move) for move in moves])

    def proj(first, last, before, extra, us):
        return project(
            place, first, groups[first:last], weight, norm_gain, heads, total, before, extra, us
        )

    state = proj(0, 4, None, 0, 6)
    *state, same, cross = proj(4, 7, state, 2, 5)
    move = lambda value, pairs: lax.ppermute(value, ("frame", "tensor"), pairs)
    same = move(same, half_pairs(1))
    cross = move(cross, half_pairs(-1))
    q, kv, raw, gathered, patch = proj(7, 8, state, 1, 2)
    far = (same, cross, move(patch, half_pairs(-1)))
    turn = 2 * mine - 1
    seen = lambda f: jnp.where((f >= 0) & (f < frames), 0.0, -1e30).astype(F32)
    bias = jnp.stack([seen(frame - turn), seen(frame + turn)])

    outs = []

    def attend(h, after):
        attended, gq, dk, dv, low, high = attention(
            bias, place, q, kv, far, out_grad, raw, norm_gain, h, after
        )
        outs.append(attended)
        same = move(low, [pair[::-1] for pair in half_pairs(1)])
        cross = move(high, [pair[::-1] for pair in half_pairs(-1)])
        return gq, dk, dv, same, cross, raw

    def reduce_x(h, grads, after):
        mine, theirs = weight_rows(h, place, len(groups), gathered, *grads, norm_gain, after)
        done.append(mine)
        came = lax.ppermute(theirs, "frame", frame_pairs(0, 0, 1))
        pieces = pair_sum(place, mine, came)
        moved = [lax.ppermute(pieces[dx], "frame", frame_pairs(dx, 0)) for dx in (1, 3, 2)]
        return pieces[0], moved

    def reduce_z(kept, moved):
        shape = kept.shape[1:]
        keep, out = on_chip(line_kernel, [kept, *moved], [(shape, F32), (shape, BF16)], name="line")
        return keep, lax.ppermute(out, "frame", frame_pairs(0, 1))

    done = []
    grads = [attend(0, norm_gain)]
    sums = []
    pairs = []
    for h in range(heads):
        if h + 1 < heads:
            grads.append(attend(h + 1, sums[-1][0] if sums else norm_gain))
        if h == 1:
            pairs.append(reduce_z(*sums[0]))
        after = done[-1] if h == 2 else pairs[-1][0] if pairs else outs[-1]
        sums.append(reduce_x(h, grads[h], after))
    for h in range(len(pairs), heads):
        pairs.append(reduce_z(*sums[h]))
    (weight_grad,) = on_chip(
        functools.partial(last_kernel, heads),
        [one[0] for one in pairs] + [one[1] for one in pairs],
        [((kinds, pairs[0][0].shape[0], local), F32)],
        name="last",
    )
    return (jnp.concatenate(outs, 1), weight_grad.transpose(1, 0, 2))


def solution(mesh):
    placed = (P(("frame", "tensor"), None), P(None, None, "tensor"), P(), P("frame", "tensor"))
    return jax.shard_map(
        per_device,
        mesh=mesh,
        in_specs=placed,
        out_specs=(P("frame", "tensor"), P("frame", None, "tensor")),
        check_vma=False,
    )
```

```python
import functools

import jax
import jax.numpy as jnp
from jax import lax
from jax.experimental import pallas as pl
from jax.experimental.pallas import tpu as pltpu
from jax.sharding import PartitionSpec as P

HEAD_DIM = 128
EPSILON = 1e-06
LOG2E = 1.4426950408889634
LIMIT = 24
FIRST = 4
F32 = jnp.float32
BF16 = jnp.bfloat16
NN = (((1,), (0,)), ((), ()))
NT = (((1,), (1,)), ((), ()))
TN = (((0,), (0,)), ((), ()))


def dot(left, right, dims=NN):
    return lax.dot_general(left, right, dims, preferred_element_type=F32)


def on_chip(kernel, ins, outs, scratch=(), limit=LIMIT, aliases=None, us=0.1, name=None):
    specs, args = [], []
    for one in ins:
        space = pltpu.VMEM
        if isinstance(one, tuple):
            one, space = one
        specs.append(pl.BlockSpec(memory_space=space))
        args.append(one)
    return pl.pallas_call(
        kernel,
        in_specs=specs,
        out_specs=[pl.BlockSpec(memory_space=(out + (pltpu.VMEM,))[2]) for out in outs],
        out_shape=[jax.ShapeDtypeStruct(*out[:2]) for out in outs],
        scratch_shapes=list(scratch),
        input_output_aliases=aliases or {},
        compiler_params=pltpu.CompilerParams(vmem_limit_bytes=limit * 1024 * 1024),
        cost_estimate=pl.CostEstimate(
            flops=int(us * 1.1e9), bytes_accessed=0, transcendentals=0
        ),
        name=name,
    )(*args)


def frame_pairs(dx, dz, dc=0):
    return [
        (zh * 8 + x * 2 + c, ((zh + dz) % 2) * 8 + ((x + dx) % 4) * 2 + (c + dc) % 2)
        for zh in range(2)
        for x in range(4)
        for c in range(2)
    ]


def tensor_pairs(dy, dz):
    return [
        (y * 2 + z, ((y + dy) % 4) * 2 + (z + dz) % 2) for y in range(4) for z in range(2)
    ]


def half_pairs(sign):
    pairs = []
    for f in range(16):
        for t in range(8):
            there = f + (sign if t // 4 else -sign)
            if 0 <= there < 16:
                pairs.append((f * 8 + t, there * 8 + t))
    return pairs


def proj_kernel(heads, groups, first, extra, place_ref, gain_ref, w_ref, *refs):
    raw_ref, *outs, x_ref = refs[sum(groups) + (1 + heads) * (first > FIRST) :]
    held, sent = outs[:heads], outs[heads:]
    at = 0
    for ref in refs[: sum(groups)]:
        x_ref[at : at + ref.shape[0]] = ref[...]
        at += ref.shape[0]
    rows = at // len(groups)
    for kind in (1, 2, 0):
        projected = dot(x_ref[...], w_ref[kind])
        for h in range(heads):
            part = projected[:, h * HEAD_DIM : (h + 1) * HEAD_DIM]
            rounded = part.astype(BF16) if kind == 2 else normed(part, gain_ref[kind : kind + 1])
            for i in range(len(groups)):
                there = pl.ds(pl.multiple_of(place_ref[first + i] * rows, rows), rows)
                here = slice(i * rows, (i + 1) * rows)
                held[h][kind, there] = rounded[here]
                if kind < 2:
                    raw_ref[kind * heads + h, there] = part[here]
            if kind > 0 and extra == 1:
                sent[0][(kind - 1) * heads + h] = rounded
    if extra == 2:
        half = raw_ref.shape[1] // 2
        for i, out in enumerate(sent):
            mine = place_ref[3] if i == 0 else 1 - place_ref[3]
            there = pl.ds(pl.multiple_of(mine * half, half), half)
            for h in range(heads):
                out[h] = held[h][1, there]
                out[heads + h] = held[h][2, there]


def normed(raw, gain):
    inverse_rms = lax.rsqrt(jnp.mean(raw * raw, axis=-1, keepdims=True) + EPSILON)
    return (raw * inverse_rms * gain).astype(BF16)


def project(place, first, groups, weight, gain, heads, total, before, extra, us):
    rows = sum(piece.shape[0] for piece in groups[0])
    depth = weight.shape[1]
    outs = [((2 * heads, total, HEAD_DIM), F32)] + [((3, total, HEAD_DIM), BF16)] * heads
    outs += [((2 * heads, total // 2 if extra == 2 else rows, HEAD_DIM), BF16)] * extra
    ins = [(place, pltpu.SMEM), gain, weight] + [piece for group in groups for piece in group]
    aliases = {}
    if before is not None:
        aliases = {len(ins) + i: i for i in range(1 + heads)}
        ins += list(before)
    counts = tuple(len(group) for group in groups)
    return on_chip(
        functools.partial(proj_kernel, heads, counts, FIRST + first, extra),
        ins,
        outs,
        [pltpu.VMEM((rows * len(groups), depth), BF16)],
        aliases=aliases,
        us=us,
        name="project",
    )


def attention_kernel(heads, block, span, bias_ref, place_ref, *refs):
    helds, refs = refs[:heads], refs[heads:]
    raw_ref, same_ref, cross_ref, patch_ref, all_grads, gain_ref = refs[:6]
    out_ref, gq_ref, dk_ref, dv_ref, low_ref, high_ref = refs[6:12]
    for h in range(heads):
        attend_head(
            h, heads, block, span, bias_ref, place_ref, helds[h], raw_ref, same_ref, cross_ref,
            patch_ref, all_grads, gain_ref, out_ref, gq_ref, dk_ref, dv_ref, low_ref, high_ref,
            *(pair.at[h % 2] for pair in refs[12:]),
        )


def attend_head(
    h, heads, block, span, bias_ref, place_ref, held_ref, raw_ref, same_ref, cross_ref, patch_ref,
    all_grads, gain_ref, out_ref, gq_ref, dk_ref, dv_ref, low_ref, high_ref, keys, values, dk_sum,
    dv_sum,
):
    rows = raw_ref.shape[1]
    half = rows // 2
    head = slice(h * HEAD_DIM, (h + 1) * HEAD_DIM)
    factor = HEAD_DIM**-0.5
    scale = factor * LOG2E
    chunk = patch_ref.shape[1]
    there = rows + half + (place_ref[FIRST + rows // chunk - 1] % (half // chunk)) * chunk
    there = pl.ds(pl.multiple_of(there, chunk), chunk)
    for kind, wide, i in ((1, keys, h), (2, values, heads + h)):
        wide[:rows, :HEAD_DIM] = held_ref[kind]
        wide[rows : rows + half, :HEAD_DIM] = same_ref[i]
        wide[rows + half :, :HEAD_DIM] = cross_ref[i]
        wide[there, :HEAD_DIM] = patch_ref[i]
    lane = lax.broadcasted_iota(jnp.int32, (2 * rows, HEAD_DIM), 1)
    values[:, HEAD_DIM:] = jnp.where(lane < 3, -1.0, 0.0).astype(BF16)
    keys[:rows, HEAD_DIM:] = jnp.zeros((rows, HEAD_DIM), BF16)
    for i in range(2):
        first = rows + i * half
        keys[first : first + half, HEAD_DIM:] = jnp.where(
            lane[:half] == 0, bias_ref[i], 0.0
        ).astype(BF16)
    lane = lane[:block]
    one = jnp.where(lane == 0, 1.0, 0.0).astype(BF16)
    for step in range(rows // block):
        here = slice(step * block, (step + 1) * block)
        query = held_ref[0, here]
        parts = [slice(j * span, (j + 1) * span) for j in range(2 * rows // span)]
        query_wide = jnp.concatenate([query, one], 1)
        scores = [dot(query_wide, keys[p], NT) for p in parts]
        peak = functools.reduce(jnp.maximum, [jnp.max(s, axis=-1, keepdims=True) for s in scores])
        peak = peak * scale
        mixed = 0.0
        weights = []
        for p, one_scores in zip(parts, scores):
            raised = jnp.exp2(one_scores * scale - peak).astype(BF16)
            weights.append(raised)
            mixed = mixed + dot(raised, values[p])
        grad = all_grads[here, head]
        inverse = -1.0 / mixed[:, HEAD_DIM : HEAD_DIM + 1]
        attended = (mixed[:, :HEAD_DIM] * inverse).astype(BF16)
        out_ref[here, head] = attended
        grad_f32 = grad.astype(F32)
        dots = jnp.sum(grad_f32 * attended.astype(F32), axis=-1, keepdims=True)
        dots_a = dots.astype(BF16)
        dots = dots - dots_a.astype(F32)
        dots_b = dots.astype(BF16)
        dots_c = (dots - dots_b.astype(F32)).astype(BF16)
        zero = jnp.zeros_like(dots_c)
        tail = jnp.where(
            lane == 0, dots_a, jnp.where(lane == 1, dots_b, jnp.where(lane == 2, dots_c, zero))
        )
        grad_wide = jnp.concatenate([grad, tail], 1)
        query_turned = (query.astype(F32) * inverse).astype(BF16).T
        grad_turned = (grad_f32 * inverse).astype(BF16).T
        query_grad = 0.0
        for p, one_weights in zip(parts, weights):
            prob_grads = dot(grad_wide, values[p], NT)
            score_grads = (one_weights.astype(F32) * prob_grads).astype(BF16)
            query_grad = query_grad + dot(score_grads, keys[p, :HEAD_DIM])
            key_part = dot(query_turned, score_grads)
            value_part = dot(grad_turned, one_weights)
            if step == 0:
                dk_sum[:, p] = key_part
                dv_sum[:, p] = value_part
            else:
                dk_sum[:, p] += key_part
                dv_sum[:, p] += value_part
        gq_ref[here, head] = norm_back(raw_ref[h, here], gain_ref[0:1], query_grad * (inverse * factor))
    dk_ref[:, head] = dk_sum[:, :rows].T * factor
    dv_ref[:, head] = dv_sum[:, :rows].T
    for out, first in ((low_ref, rows), (high_ref, rows + half)):
        out[h] = (dk_sum[:, first : first + half].T * factor).astype(BF16)
        out[heads + h] = dv_sum[:, first : first + half].T.astype(BF16)


def norm_back(raw, gain, grad):
    inverse_rms = lax.rsqrt(jnp.mean(raw * raw, axis=-1, keepdims=True) + EPSILON)
    weighted = grad * gain
    unit = raw * inverse_rms
    inner = jnp.mean(unit * weighted, axis=-1, keepdims=True)
    return (inverse_rms * (weighted - unit * inner)).astype(BF16)


def attention(bias, place, helds, raw, far, out_grad, gain, block=512, span=512):
    heads = len(helds)
    rows = raw.shape[1]
    width = heads * HEAD_DIM
    return on_chip(
        functools.partial(attention_kernel, heads, block, span),
        [(bias, pltpu.SMEM), (place, pltpu.SMEM), *helds, raw, *far, out_grad, gain],
        [((rows, width), BF16)] * 2
        + [((rows, width), F32)] * 2
        + [((2 * heads, rows // 2, HEAD_DIM), BF16)] * 2,
        [pltpu.VMEM((2, 2 * rows, 2 * HEAD_DIM), BF16)] * 2
        + [pltpu.VMEM((2, HEAD_DIM, 2 * rows), F32)] * 2,
        us=33,
        name="attention",
    )


def split_rows(count, place_ref, straight, g, pieces, mine_ref, theirs_ref):
    chunk = straight.shape[0] // count
    for i in range(count):
        there = pl.ds(pl.multiple_of(place_ref[FIRST + i] * chunk, chunk), chunk)
        g[i * chunk : (i + 1) * chunk] = straight[there]
    blocks, rows, _ = mine_ref.shape
    low = place_ref[2] == 0
    for b in range(blocks):
        columns = slice(2 * b * rows, 2 * (b + 1) * rows)
        x = jnp.concatenate([piece[:, columns] for piece in pieces], 0)
        product = dot(x, g[...], TN).astype(BF16)
        mine_ref[b] = jnp.where(low, product[:rows], product[rows:])
        theirs_ref[b] = jnp.where(low, product[rows:], product[:rows])


def query_kernel(count, place_ref, gq_ref, *refs):
    mine_ref, theirs_ref, g = refs[-3:]
    split_rows(count, place_ref, gq_ref, g, refs[:-3], mine_ref, theirs_ref)


def key_value_kernel(
    count, heads, place_ref, dk_ref, dv_ref, same_ref, cross_ref, raw_ref, gain_ref, after_ref, *refs
):
    mine_ref, theirs_ref, straight, g = refs[-4:]
    half = dk_ref.shape[0] // 2
    for i, came in enumerate((same_ref, cross_ref)):
        mine = place_ref[3] if i == 0 else 1 - place_ref[3]
        rows = pl.ds(pl.multiple_of(mine * half, half), half)
        for h in range(heads):
            head = slice(h * HEAD_DIM, (h + 1) * HEAD_DIM)
            there = slice((heads + h) * HEAD_DIM, (heads + h + 1) * HEAD_DIM)
            dk = dk_ref[rows, head] + came[h].astype(F32)
            dv = dv_ref[rows, head] + came[heads + h].astype(F32)
            straight[rows, head] = norm_back(raw_ref[heads + h, rows], gain_ref[1:2], dk)
            straight[rows, there] = dv.astype(BF16)
    split_rows(count, place_ref, straight, g, refs[:-4], mine_ref, theirs_ref)


def weight_rows(kernel, groups, place, ins, total, width, held, us, name):
    pieces = [piece for group in groups for piece in group]
    out = ((8, pieces[0].shape[1] // 16, width), BF16)
    return on_chip(
        kernel,
        [(place, pltpu.SMEM), *ins, *pieces],
        [out, out],
        [pltpu.VMEM((total, width), BF16)] * held,
        us=us,
        name=name,
    )


def pair_kernel(place_ref, mine_q, came_q, mine_kv, came_kv, *outs):
    zh, x = place_ref[0], place_ref[1]
    rows = mine_q.shape[1] // 2
    along_x, (stay, leave) = outs[:4], outs[4:]
    at = 0
    for mine, came in ((mine_q, came_q), (mine_kv, came_kv)):
        columns = slice(at, at + mine.shape[2])
        at += mine.shape[2]
        for dx in range(4):
            for dz in range(2):
                b = ((zh + dz) % 2) * 4 + (x + dx) % 4
                both = (mine[b].astype(F32) + came[b].astype(F32)).astype(BF16)
                along_x[dx][dz, :, columns] = both[:rows]
                (leave if dz else stay)[dx, :, columns] = both[rows:]


def after_x_kernel(a_ref, b_ref, c_ref, d_ref, keep_ref, send_ref):
    for i, out in enumerate((keep_ref, send_ref)):
        summed = a_ref[i].astype(F32) + b_ref[i].astype(F32)
        summed = summed + c_ref[i].astype(F32) + d_ref[i].astype(F32)
        out[...] = summed.astype(out.dtype)


def after_z_kernel(stay_ref, came_ref, *outs):
    for dx, out in enumerate(outs):
        out[...] = (stay_ref[dx].astype(F32) + came_ref[dx].astype(F32)).astype(out.dtype)


def last_kernel(keep_x, came_x, keep_z, a_ref, b_ref, c_ref, out):
    rows = keep_x.shape[0]
    top = keep_x[...] + came_x[...].astype(F32)
    bottom = keep_z[...] + a_ref[...].astype(F32)
    bottom = bottom + b_ref[...].astype(F32) + c_ref[...].astype(F32)
    width = out.shape[2]
    for kind in range(3):
        columns = slice(kind * width, (kind + 1) * width)
        out[kind, :rows] = top[:, columns]
        out[kind, rows:] = bottom[:, columns]


def halves_kernel(first_ref, last_ref, first_half, last_half):
    cut = first_half.shape[0]
    first_half[...] = first_ref[:cut]
    last_half[...] = last_ref[cut:]


def per_device(hidden, qkv_weight, norm_gain, out_grad):
    depth, kinds, local = qkv_weight.shape
    heads = local // HEAD_DIM
    chunk = hidden.shape[0]
    total = chunk * lax.axis_size("tensor")
    half = total // 2
    frame = lax.axis_index("frame").astype(jnp.int32)
    frames = lax.axis_size("frame")
    tensor = lax.axis_index("tensor").astype(jnp.int32)
    zh, x, core = frame // 8, (frame // 2) % 4, frame % 2
    y, zl = tensor // 2, tensor % 2
    def at(dy, dz):
        return ((y + dy) % 4) * 2 + (zl + dz) % 2

    weight = qkv_weight.transpose(1, 0, 2)

    send = lambda value, dy, dz: lax.ppermute(value, "tensor", tensor_pairs(dy, dz))
    cut = chunk // 2
    below = send(hidden, 1, 0)
    above = send(hidden, -1, 0)
    side = send(hidden, 0, 1)
    far = send(above, -1, 0)
    side_above = send(above, 0, 1)
    side_below = send(side, 1, 0)
    first_half, last_half = on_chip(
        halves_kernel, [side_above, far], [((cut, depth), BF16)] * 2, name="halves"
    )
    side_far = (send(first_half, -1, 0), send(last_half, 0, 1))
    groups = [(hidden,), (below,), (above,), (side,), (far,), (side_below,), (side_above,), side_far]
    moves = [(0, 0), (-1, 0), (1, 0), (0, 1), (2, 0), (-1, 1), (1, 1), (2, 1)]
    mine = y // 2
    place = jnp.stack([zh, x, core, mine] + [at(*move) for move in moves])

    def proj(first, last, before, extra, us):
        return project(
            place, first, groups[first:last], weight, norm_gain, heads, total, before, extra, us
        )

    state = proj(0, 4, None, 0, 6)
    *state, same, cross = proj(4, 7, state, 2, 5)
    move = lambda value, pairs: lax.ppermute(value, ("frame", "tensor"), pairs)
    same = move(same, half_pairs(1))
    cross = move(cross, half_pairs(-1))
    raw, *held, patch = proj(7, 8, state, 1, 2)
    far = (same, cross, move(patch, half_pairs(-1)))
    turn = 2 * mine - 1
    seen = lambda f: jnp.where((f >= 0) & (f < frames), 0.0, -1e30).astype(F32)
    bias = jnp.stack([seen(frame - turn), seen(frame + turn)])

    attended, gq, dk, dv, low, high = attention(
        bias, place, held, raw, far, out_grad, norm_gain
    )
    same = move(low, [pair[::-1] for pair in half_pairs(1)])
    cross = move(high, [pair[::-1] for pair in half_pairs(-1)])
    count = len(groups)
    swap = lambda value: lax.ppermute(value, "frame", frame_pairs(0, 0, 1))
    mine_q, theirs_q = weight_rows(
        functools.partial(query_kernel, count), groups, place, [gq], total, local, 1, 5, "query"
    )
    mine_kv, theirs_kv = weight_rows(
        functools.partial(key_value_kernel, count, heads),
        groups,
        place,
        [dk, dv, same, cross, raw, norm_gain, (mine_q, pl.ANY)],
        total,
        2 * local,
        2,
        8,
        "key_value",
    )
    rows = mine_q.shape[1] // 2
    wide = kinds * local
    piece = ((2, rows, wide), BF16)
    line = ((4, rows, wide), BF16)
    *along_x, stay, leave = on_chip(
        pair_kernel,
        [(place, pltpu.SMEM), mine_q, swap(theirs_q), mine_kv, swap(theirs_kv)],
        [piece] * 4 + [line] * 2,
        name="pair",
    )
    shift = lambda value, dx, dz: lax.ppermute(value, "frame", frame_pairs(dx, dz))
    came = shift(leave, 0, 1)
    moved = [shift(along_x[dx], dx, 0) for dx in (1, 3, 2)]
    one = (rows, wide)
    keep_x, send_x = on_chip(
        after_x_kernel, [along_x[0], *moved], [(one, F32), (one, BF16)], name="after_x"
    )
    came_x = shift(send_x, 0, 1)
    keep_z, *send_z = on_chip(
        after_z_kernel, [stay, came], [(one, F32)] + [(one, BF16)] * 3, name="after_z"
    )
    came_z = [shift(send_z[dx - 1], dx, 0) for dx in (1, 3, 2)]
    (weight_grad,) = on_chip(
        last_kernel,
        [keep_x, came_x, keep_z, *came_z],
        [((kinds, 2 * rows, local), F32)],
        name="last",
    )
    return (attended, weight_grad.transpose(1, 0, 2))


def solution(mesh):
    placed = (P(("frame", "tensor"), None), P(None, None, "tensor"), P(), P("frame", "tensor"))
    return jax.shard_map(
        per_device,
        mesh=mesh,
        in_specs=placed,
        out_specs=(P("frame", "tensor"), P("frame", None, "tensor")),
        check_vma=False,
    )
```

```python
import functools

import jax
import jax.numpy as jnp
from jax import lax
from jax.experimental import pallas as pl
from jax.experimental.pallas import tpu as pltpu
from jax.sharding import PartitionSpec as P

HEAD_DIM = 128
EPSILON = 1e-06
LOG2E = 1.4426950408889634
LIMIT = 24
FIRST = 4
F32 = jnp.float32
BF16 = jnp.bfloat16
NN = (((1,), (0,)), ((), ()))
NT = (((1,), (1,)), ((), ()))
TN = (((0,), (0,)), ((), ()))


def dot(left, right, dims=NN):
    return lax.dot_general(left, right, dims, preferred_element_type=F32)


def on_chip(kernel, ins, outs, scratch=(), limit=LIMIT, aliases=None, us=0.1, name=None):
    specs, args = [], []
    for one in ins:
        space = pltpu.VMEM
        if isinstance(one, tuple):
            one, space = one
        specs.append(pl.BlockSpec(memory_space=space))
        args.append(one)
    return pl.pallas_call(
        kernel,
        in_specs=specs,
        out_specs=[pl.BlockSpec(memory_space=(out + (pltpu.VMEM,))[2]) for out in outs],
        out_shape=[jax.ShapeDtypeStruct(*out[:2]) for out in outs],
        scratch_shapes=list(scratch),
        input_output_aliases=aliases or {},
        compiler_params=pltpu.CompilerParams(vmem_limit_bytes=limit * 1024 * 1024),
        cost_estimate=pl.CostEstimate(
            flops=int(us * 1.1e9), bytes_accessed=0, transcendentals=0
        ),
        name=name,
    )(*args)


def frame_pairs(dx, dz, dc=0):
    return [
        (zh * 8 + x * 2 + c, ((zh + dz) % 2) * 8 + ((x + dx) % 4) * 2 + (c + dc) % 2)
        for zh in range(2)
        for x in range(4)
        for c in range(2)
    ]


def tensor_pairs(dy, dz):
    return [
        (y * 2 + z, ((y + dy) % 4) * 2 + (z + dz) % 2) for y in range(4) for z in range(2)
    ]


def half_pairs(sign):
    pairs = []
    for f in range(16):
        for t in range(8):
            there = f + (sign if t // 4 else -sign)
            if 0 <= there < 16:
                pairs.append((f * 8 + t, there * 8 + t))
    return pairs


def proj_kernel(heads, groups, first, extra, place_ref, gain_ref, w_ref, *refs):
    raw_ref, *outs, x_ref = refs[sum(groups) + (1 + heads) * (first > FIRST) :]
    held, sent = outs[:heads], outs[heads:]
    at = 0
    for ref in refs[: sum(groups)]:
        x_ref[at : at + ref.shape[0]] = ref[...]
        at += ref.shape[0]
    rows = at // len(groups)
    for kind in (1, 2, 0):
        projected = dot(x_ref[...], w_ref[kind])
        for h in range(heads):
            part = projected[:, h * HEAD_DIM : (h + 1) * HEAD_DIM]
            rounded = part.astype(BF16) if kind == 2 else normed(part, gain_ref[kind : kind + 1])
            for i in range(len(groups)):
                there = pl.ds(pl.multiple_of(place_ref[first + i] * rows, rows), rows)
                here = slice(i * rows, (i + 1) * rows)
                held[h][kind, there] = rounded[here]
                if kind < 2:
                    raw_ref[kind * heads + h, there] = part[here]
    if extra:
        half = raw_ref.shape[1] // 2
        for i, out in enumerate(sent):
            mine = place_ref[3] if i == 0 else 1 - place_ref[3]
            there = pl.ds(pl.multiple_of(mine * half, half), half)
            for h in range(heads):
                out[h] = held[h][1, there]
                out[heads + h] = held[h][2, there]


def normed(raw, gain):
    inverse_rms = lax.rsqrt(jnp.mean(raw * raw, axis=-1, keepdims=True) + EPSILON)
    return (raw * inverse_rms * gain).astype(BF16)


def project(place, first, groups, weight, gain, heads, total, before, extra, us):
    rows = sum(piece.shape[0] for piece in groups[0])
    depth = weight.shape[1]
    outs = [((2 * heads, total, HEAD_DIM), F32)] + [((3, total, HEAD_DIM), BF16)] * heads
    outs += [((2 * heads, total // 2, HEAD_DIM), BF16)] * extra
    ins = [(place, pltpu.SMEM), gain, weight] + [piece for group in groups for piece in group]
    aliases = {}
    if before is not None:
        aliases = {len(ins) + i: i for i in range(1 + heads)}
        ins += list(before)
    counts = tuple(len(group) for group in groups)
    return on_chip(
        functools.partial(proj_kernel, heads, counts, FIRST + first, extra),
        ins,
        outs,
        [pltpu.VMEM((rows * len(groups), depth), BF16)],
        aliases=aliases,
        us=us,
        name="project",
    )


def own_kernel(heads, block, span, *refs):
    helds, (raised_ref, first_ref, values) = refs[:heads], refs[heads:]
    rows = helds[0].shape[1]
    scale = HEAD_DIM**-0.5 * LOG2E
    lane = lax.broadcasted_iota(jnp.int32, (rows, HEAD_DIM), 1)
    parts = [slice(j * span, (j + 1) * span) for j in range(rows // span)]
    for h, held_ref in enumerate(helds):
        wide = values.at[h % 2]
        wide[:, :HEAD_DIM] = held_ref[2]
        wide[:, HEAD_DIM:] = jnp.where(lane < 3, -1.0, 0.0).astype(BF16)
        for step in range(rows // block):
            here = slice(step * block, (step + 1) * block)
            query = held_ref[0, here]
            scores = [dot(query, held_ref[1, p], NT) for p in parts]
            peak = functools.reduce(
                jnp.maximum, [jnp.max(s, axis=-1, keepdims=True) for s in scores]
            )
            peak = peak * scale
            mixed = 0.0
            for p, one_scores in zip(parts, scores):
                raised = jnp.exp2(one_scores * scale - peak).astype(BF16)
                raised_ref[h, here, p] = raised
                mixed = mixed + dot(raised, wide[p])
            first_ref[h, here, :HEAD_DIM] = mixed[:, :HEAD_DIM]
            first_ref[h, here, HEAD_DIM:] = jnp.where(
                lane[:block] == 1, peak, mixed[:, HEAD_DIM:]
            )


def own_attention(helds, block=512, span=512):
    heads, rows = len(helds), helds[0].shape[1]
    return on_chip(
        functools.partial(own_kernel, heads, block, span),
        helds,
        [((heads, rows, rows), BF16), ((heads, rows, 2 * HEAD_DIM), F32)],
        [pltpu.VMEM((2, rows, 2 * HEAD_DIM), BF16)],
        us=11,
        name="own_attention",
    )


def attention_kernel(heads, block, span, bias_ref, *refs):
    helds, refs = refs[:heads], refs[heads:]
    raw_ref, same_ref, cross_ref, raised_ref, first_ref, all_grads, gain_ref = refs[:7]
    out_ref, gq_ref, dk_ref, dv_ref, low_ref, high_ref = refs[7:13]
    for h in range(heads):
        attend_head(
            h, heads, block, span, bias_ref, helds[h], raw_ref, same_ref, cross_ref, raised_ref,
            first_ref, all_grads, gain_ref, out_ref, gq_ref, dk_ref, dv_ref, low_ref, high_ref,
            *(pair.at[h % 2] for pair in refs[13:]),
        )


def attend_head(
    h, heads, block, span, bias_ref, held_ref, raw_ref, same_ref, cross_ref, raised_ref, first_ref,
    all_grads, gain_ref, out_ref, gq_ref, dk_ref, dv_ref, low_ref, high_ref, keys, values, dk_sum,
    dv_sum,
):
    rows = raw_ref.shape[1]
    half = rows // 2
    head = slice(h * HEAD_DIM, (h + 1) * HEAD_DIM)
    factor = HEAD_DIM**-0.5
    scale = factor * LOG2E
    for kind, wide, i in ((1, keys, h), (2, values, heads + h)):
        wide[:rows, :HEAD_DIM] = held_ref[kind]
        wide[rows : rows + half, :HEAD_DIM] = same_ref[i]
        wide[rows + half :, :HEAD_DIM] = cross_ref[i]
    lane = lax.broadcasted_iota(jnp.int32, (2 * rows, HEAD_DIM), 1)
    values[:, HEAD_DIM:] = jnp.where(lane < 3, -1.0, 0.0).astype(BF16)
    for i in range(2):
        first = rows + i * half
        keys[first : first + half, HEAD_DIM:] = jnp.where(
            lane[:half] == 0, bias_ref[i], 0.0
        ).astype(BF16)
    lane = lane[:block]
    one = jnp.where(lane == 0, 1.0, 0.0).astype(BF16)
    parts = [slice(j * span, (j + 1) * span) for j in range(2 * rows // span)]
    own = len(parts) // 2
    for step in range(rows // block):
        here = slice(step * block, (step + 1) * block)
        query = held_ref[0, here]
        query_wide = jnp.concatenate([query, one], 1)
        scores = [dot(query_wide, keys[p], NT) for p in parts[own:]]
        begun = first_ref[h, here]
        own_peak = begun[:, HEAD_DIM + 1 : HEAD_DIM + 2]
        peak = functools.reduce(jnp.maximum, [jnp.max(s, axis=-1, keepdims=True) for s in scores])
        peak = jnp.maximum(peak * scale, own_peak)
        drop = jnp.exp2(own_peak - peak)
        mixed = begun * drop
        weights = [raised_ref[h, here, p] for p in parts[:own]]
        for p, one_scores in zip(parts[own:], scores):
            raised = jnp.exp2(one_scores * scale - peak).astype(BF16)
            weights.append(raised)
            mixed = mixed + dot(raised, values[p])
        inverse = -1.0 / mixed[:, HEAD_DIM : HEAD_DIM + 1]
        grad = all_grads[here, head]
        attended = (mixed[:, :HEAD_DIM] * inverse).astype(BF16)
        out_ref[here, head] = attended
        grad_f32 = grad.astype(F32)
        dots = jnp.sum(grad_f32 * attended.astype(F32), axis=-1, keepdims=True)
        dots_a = dots.astype(BF16)
        dots = dots - dots_a.astype(F32)
        dots_b = dots.astype(BF16)
        dots_c = (dots - dots_b.astype(F32)).astype(BF16)
        zero = jnp.zeros_like(dots_c)
        tail = jnp.where(
            lane == 0, dots_a, jnp.where(lane == 1, dots_b, jnp.where(lane == 2, dots_c, zero))
        )
        grad_wide = jnp.concatenate([grad, tail], 1)
        query_f32 = query.astype(F32)
        total = 0.0
        for factors, which in ((inverse * drop, range(own)), (inverse, range(own, 2 * own))):
            query_turned = (query_f32 * factors).astype(BF16).T
            grad_turned = (grad_f32 * factors).astype(BF16).T
            query_grad = 0.0
            for j in which:
                p = parts[j]
                prob_grads = dot(grad_wide, values[p], NT)
                score_grads = (weights[j].astype(F32) * prob_grads).astype(BF16)
                query_grad = query_grad + dot(score_grads, keys[p, :HEAD_DIM])
                key_part = dot(query_turned, score_grads)
                value_part = dot(grad_turned, weights[j])
                if step == 0:
                    dk_sum[:, p] = key_part
                    dv_sum[:, p] = value_part
                else:
                    dk_sum[:, p] += key_part
                    dv_sum[:, p] += value_part
            total = total + query_grad * (factors * factor)
        gq_ref[here, head] = norm_back(raw_ref[h, here], gain_ref[0:1], total)
    dk_ref[:, head] = dk_sum[:, :rows].T * factor
    dv_ref[:, head] = dv_sum[:, :rows].T
    for out, first in ((low_ref, rows), (high_ref, rows + half)):
        out[h] = (dk_sum[:, first : first + half].T * factor).astype(BF16)
        out[heads + h] = dv_sum[:, first : first + half].T.astype(BF16)


def norm_back(raw, gain, grad):
    inverse_rms = lax.rsqrt(jnp.mean(raw * raw, axis=-1, keepdims=True) + EPSILON)
    weighted = grad * gain
    unit = raw * inverse_rms
    inner = jnp.mean(unit * weighted, axis=-1, keepdims=True)
    return (inverse_rms * (weighted - unit * inner)).astype(BF16)


def attention(bias, helds, raw, far, begun, out_grad, gain, block=512, span=512):
    heads = len(helds)
    rows = raw.shape[1]
    width = heads * HEAD_DIM
    return on_chip(
        functools.partial(attention_kernel, heads, block, span),
        [(bias, pltpu.SMEM), *helds, raw, *far, *begun, out_grad, gain],
        [((rows, width), BF16)] * 2
        + [((rows, width), F32)] * 2
        + [((2 * heads, rows // 2, HEAD_DIM), BF16)] * 2,
        [pltpu.VMEM((2, 2 * rows, 2 * HEAD_DIM), BF16)] * 2
        + [pltpu.VMEM((2, HEAD_DIM, 2 * rows), F32)] * 2,
        us=23,
        name="attention",
    )


def split_rows(count, place_ref, straight, g, pieces, mine_ref, theirs_ref):
    chunk = straight.shape[0] // count
    for i in range(count):
        there = pl.ds(pl.multiple_of(place_ref[FIRST + i] * chunk, chunk), chunk)
        g[i * chunk : (i + 1) * chunk] = straight[there]
    blocks, rows, _ = mine_ref.shape
    low = place_ref[2] == 0
    for b in range(blocks):
        columns = slice(2 * b * rows, 2 * (b + 1) * rows)
        x = jnp.concatenate([piece[:, columns] for piece in pieces], 0)
        product = dot(x, g[...], TN).astype(BF16)
        mine_ref[b] = jnp.where(low, product[:rows], product[rows:])
        theirs_ref[b] = jnp.where(low, product[rows:], product[:rows])


def query_kernel(count, place_ref, gq_ref, *refs):
    mine_ref, theirs_ref, g = refs[-3:]
    split_rows(count, place_ref, gq_ref, g, refs[:-3], mine_ref, theirs_ref)


def key_value_kernel(
    count, heads, place_ref, dk_ref, dv_ref, same_ref, cross_ref, raw_ref, gain_ref, after_ref, *refs
):
    mine_ref, theirs_ref, straight, g = refs[-4:]
    half = dk_ref.shape[0] // 2
    for i, came in enumerate((same_ref, cross_ref)):
        mine = place_ref[3] if i == 0 else 1 - place_ref[3]
        rows = pl.ds(pl.multiple_of(mine * half, half), half)
        for h in range(heads):
            head = slice(h * HEAD_DIM, (h + 1) * HEAD_DIM)
            there = slice((heads + h) * HEAD_DIM, (heads + h + 1) * HEAD_DIM)
            dk = dk_ref[rows, head] + came[h].astype(F32)
            dv = dv_ref[rows, head] + came[heads + h].astype(F32)
            straight[rows, head] = norm_back(raw_ref[heads + h, rows], gain_ref[1:2], dk)
            straight[rows, there] = dv.astype(BF16)
    split_rows(count, place_ref, straight, g, refs[:-4], mine_ref, theirs_ref)


def weight_rows(kernel, groups, place, ins, total, width, held, us, name):
    pieces = [piece for group in groups for piece in group]
    out = ((8, pieces[0].shape[1] // 16, width), BF16)
    return on_chip(
        kernel,
        [(place, pltpu.SMEM), *ins, *pieces],
        [out, out],
        [pltpu.VMEM((total, width), BF16)] * held,
        us=us,
        name=name,
    )


def pair_kernel(place_ref, mine_q, came_q, mine_kv, came_kv, *outs):
    zh, x = place_ref[0], place_ref[1]
    rows = mine_q.shape[1] // 2
    along_x, (stay, leave) = outs[:4], outs[4:]
    at = 0
    for mine, came in ((mine_q, came_q), (mine_kv, came_kv)):
        columns = slice(at, at + mine.shape[2])
        at += mine.shape[2]
        for dx in range(4):
            for dz in range(2):
                b = ((zh + dz) % 2) * 4 + (x + dx) % 4
                both = (mine[b].astype(F32) + came[b].astype(F32)).astype(BF16)
                along_x[dx][dz, :, columns] = both[:rows]
                (leave if dz else stay)[dx, :, columns] = both[rows:]


def after_x_kernel(a_ref, b_ref, c_ref, d_ref, keep_ref, send_ref):
    for i, out in enumerate((keep_ref, send_ref)):
        summed = a_ref[i].astype(F32) + b_ref[i].astype(F32)
        summed = summed + c_ref[i].astype(F32) + d_ref[i].astype(F32)
        out[...] = summed.astype(out.dtype)


def after_z_kernel(stay_ref, came_ref, *outs):
    for dx, out in enumerate(outs):
        out[...] = (stay_ref[dx].astype(F32) + came_ref[dx].astype(F32)).astype(out.dtype)


def last_kernel(keep_x, came_x, keep_z, a_ref, b_ref, c_ref, out):
    rows = keep_x.shape[0]
    top = keep_x[...] + came_x[...].astype(F32)
    bottom = keep_z[...] + a_ref[...].astype(F32)
    bottom = bottom + b_ref[...].astype(F32) + c_ref[...].astype(F32)
    width = out.shape[2]
    for kind in range(3):
        columns = slice(kind * width, (kind + 1) * width)
        out[kind, :rows] = top[:, columns]
        out[kind, rows:] = bottom[:, columns]


def halves_kernel(first_ref, last_ref, first_half, last_half):
    cut = first_half.shape[0]
    first_half[...] = first_ref[:cut]
    last_half[...] = last_ref[cut:]


def per_device(hidden, qkv_weight, norm_gain, out_grad):
    depth, kinds, local = qkv_weight.shape
    heads = local // HEAD_DIM
    chunk = hidden.shape[0]
    total = chunk * lax.axis_size("tensor")
    half = total // 2
    frame = lax.axis_index("frame").astype(jnp.int32)
    frames = lax.axis_size("frame")
    tensor = lax.axis_index("tensor").astype(jnp.int32)
    zh, x, core = frame // 8, (frame // 2) % 4, frame % 2
    y, zl = tensor // 2, tensor % 2
    def at(dy, dz):
        return ((y + dy) % 4) * 2 + (zl + dz) % 2

    weight = qkv_weight.transpose(1, 0, 2)

    send = lambda value, dy, dz: lax.ppermute(value, "tensor", tensor_pairs(dy, dz))
    cut = chunk // 2
    below = send(hidden, 1, 0)
    above = send(hidden, -1, 0)
    side = send(hidden, 0, 1)
    far = send(above, -1, 0)
    side_above = send(above, 0, 1)
    side_below = send(side, 1, 0)
    first_half, last_half = on_chip(
        halves_kernel, [side_above, far], [((cut, depth), BF16)] * 2, name="halves"
    )
    side_far = (send(first_half, -1, 0), send(last_half, 0, 1))
    groups = [(hidden,), (below,), (above,), (side,), (far,), (side_below,), (side_above,), side_far]
    moves = [(0, 0), (-1, 0), (1, 0), (0, 1), (2, 0), (-1, 1), (1, 1), (2, 1)]
    mine = y // 2
    place = jnp.stack([zh, x, core, mine] + [at(*move) for move in moves])

    def proj(first, last, before, extra, us):
        return project(
            place, first, groups[first:last], weight, norm_gain, heads, total, before, extra, us
        )

    move = lambda value, pairs: lax.ppermute(value, ("frame", "tensor"), pairs)
    state = proj(0, 4, None, 0, 6)
    state = proj(4, 7, state, 0, 5)
    raw, *held, same, cross = proj(7, 8, state, 2, 2)
    far = (move(same, half_pairs(1)), move(cross, half_pairs(-1)))
    turn = 2 * mine - 1
    seen = lambda f: jnp.where((f >= 0) & (f < frames), 0.0, -1e30).astype(F32)
    bias = jnp.stack([seen(frame - turn), seen(frame + turn)])

    begun = own_attention(held)
    attended, gq, dk, dv, low, high = attention(bias, held, raw, far, begun, out_grad, norm_gain)
    same = move(low, [pair[::-1] for pair in half_pairs(1)])
    cross = move(high, [pair[::-1] for pair in half_pairs(-1)])
    count = len(groups)
    swap = lambda value: lax.ppermute(value, "frame", frame_pairs(0, 0, 1))
    mine_q, theirs_q = weight_rows(
        functools.partial(query_kernel, count), groups, place, [gq], total, local, 1, 5, "query"
    )
    mine_kv, theirs_kv = weight_rows(
        functools.partial(key_value_kernel, count, heads),
        groups,
        place,
        [dk, dv, same, cross, raw, norm_gain, (mine_q, pl.ANY)],
        total,
        2 * local,
        2,
        8,
        "key_value",
    )
    rows = mine_q.shape[1] // 2
    wide = kinds * local
    piece = ((2, rows, wide), BF16)
    line = ((4, rows, wide), BF16)
    *along_x, stay, leave = on_chip(
        pair_kernel,
        [(place, pltpu.SMEM), mine_q, swap(theirs_q), mine_kv, swap(theirs_kv)],
        [piece] * 4 + [line] * 2,
        name="pair",
    )
    shift = lambda value, dx, dz: lax.ppermute(value, "frame", frame_pairs(dx, dz))
    came = shift(leave, 0, 1)
    moved = [shift(along_x[dx], dx, 0) for dx in (1, 3, 2)]
    one = (rows, wide)
    keep_x, send_x = on_chip(
        after_x_kernel, [along_x[0], *moved], [(one, F32), (one, BF16)], name="after_x"
    )
    came_x = shift(send_x, 0, 1)
    keep_z, *send_z = on_chip(
        after_z_kernel, [stay, came], [(one, F32)] + [(one, BF16)] * 3, name="after_z"
    )
    came_z = [shift(send_z[dx - 1], dx, 0) for dx in (1, 3, 2)]
    (weight_grad,) = on_chip(
        last_kernel,
        [keep_x, came_x, keep_z, *came_z],
        [((kinds, 2 * rows, local), F32)],
        name="last",
    )
    return (attended, weight_grad.transpose(1, 0, 2))


def solution(mesh):
    placed = (P(("frame", "tensor"), None), P(None, None, "tensor"), P(), P("frame", "tensor"))
    return jax.shard_map(
        per_device,
        mesh=mesh,
        in_specs=placed,
        out_specs=(P("frame", "tensor"), P("frame", None, "tensor")),
        check_vma=False,
    )
```

```python
import functools

import jax
import jax.numpy as jnp
from jax import lax
from jax.experimental import pallas as pl
from jax.experimental.pallas import tpu as pltpu
from jax.sharding import PartitionSpec as P

HEAD_DIM = 128
EPSILON = 1e-06
LOG2E = 1.4426950408889634
LIMIT = 24
FIRST = 4
F32 = jnp.float32
BF16 = jnp.bfloat16
NN = (((1,), (0,)), ((), ()))
NT = (((1,), (1,)), ((), ()))
TN = (((0,), (0,)), ((), ()))


def dot(left, right, dims=NN):
    return lax.dot_general(left, right, dims, preferred_element_type=F32)


def on_chip(kernel, ins, outs, scratch=(), limit=LIMIT, aliases=None, us=0.1, name=None):
    specs, args = [], []
    for one in ins:
        space = pltpu.VMEM
        if isinstance(one, tuple):
            one, space = one
        specs.append(pl.BlockSpec(memory_space=space))
        args.append(one)
    return pl.pallas_call(
        kernel,
        in_specs=specs,
        out_specs=[pl.BlockSpec(memory_space=(out + (pltpu.VMEM,))[2]) for out in outs],
        out_shape=[jax.ShapeDtypeStruct(*out[:2]) for out in outs],
        scratch_shapes=list(scratch),
        input_output_aliases=aliases or {},
        compiler_params=pltpu.CompilerParams(vmem_limit_bytes=limit * 1024 * 1024),
        cost_estimate=pl.CostEstimate(
            flops=int(us * 1.1e9), bytes_accessed=0, transcendentals=0
        ),
        name=name,
    )(*args)


def frame_pairs(dx, dz, dc=0):
    return [
        (zh * 8 + x * 2 + c, ((zh + dz) % 2) * 8 + ((x + dx) % 4) * 2 + (c + dc) % 2)
        for zh in range(2)
        for x in range(4)
        for c in range(2)
    ]


def tensor_pairs(dy, dz):
    return [
        (y * 2 + z, ((y + dy) % 4) * 2 + (z + dz) % 2) for y in range(4) for z in range(2)
    ]


def half_pairs(sign):
    pairs = []
    for f in range(16):
        for t in range(8):
            there = f + (sign if t // 4 else -sign)
            if 0 <= there < 16:
                pairs.append((f * 8 + t, there * 8 + t))
    return pairs


def proj_kernel(heads, groups, first, extra, place_ref, gain_ref, w_ref, *refs):
    raw_ref, *outs, x_ref = refs[sum(groups) + (1 + heads) * (first > FIRST) :]
    held, sent = outs[:heads], outs[heads:]
    at = 0
    for ref in refs[: sum(groups)]:
        x_ref[at : at + ref.shape[0]] = ref[...]
        at += ref.shape[0]
    rows = at // len(groups)
    for kind in (1, 2, 0):
        projected = dot(x_ref[...], w_ref[kind])
        for h in range(heads):
            part = projected[:, h * HEAD_DIM : (h + 1) * HEAD_DIM]
            rounded = part.astype(BF16) if kind == 2 else normed(part, gain_ref[kind : kind + 1])
            for i in range(len(groups)):
                there = pl.ds(pl.multiple_of(place_ref[first + i] * rows, rows), rows)
                here = slice(i * rows, (i + 1) * rows)
                held[h][kind, there] = rounded[here]
                if kind < 2:
                    raw_ref[kind * heads + h, there] = part[here]
    if extra:
        half = raw_ref.shape[1] // 2
        for i, out in enumerate(sent):
            mine = place_ref[3] if i == 0 else 1 - place_ref[3]
            there = pl.ds(pl.multiple_of(mine * half, half), half)
            for h in range(heads):
                out[h] = held[h][1, there]
                out[heads + h] = held[h][2, there]


def normed(raw, gain):
    inverse_rms = lax.rsqrt(jnp.mean(raw * raw, axis=-1, keepdims=True) + EPSILON)
    return (raw * inverse_rms * gain).astype(BF16)


def project(place, first, groups, weight, gain, heads, total, before, extra, us):
    rows = sum(piece.shape[0] for piece in groups[0])
    depth = weight.shape[1]
    outs = [((2 * heads, total, HEAD_DIM), F32)] + [((3, total, HEAD_DIM), BF16)] * heads
    outs += [((2 * heads, total // 2, HEAD_DIM), BF16)] * extra
    ins = [(place, pltpu.SMEM), gain, weight] + [piece for group in groups for piece in group]
    aliases = {}
    if before is not None:
        aliases = {len(ins) + i: i for i in range(1 + heads)}
        ins += list(before)
    counts = tuple(len(group) for group in groups)
    return on_chip(
        functools.partial(proj_kernel, heads, counts, FIRST + first, extra),
        ins,
        outs,
        [pltpu.VMEM((rows * len(groups), depth), BF16)],
        aliases=aliases,
        us=us,
        name="project",
    )


def own_kernel(heads, block, span, *refs):
    helds, (raised_ref, first_ref, values) = refs[:heads], refs[heads:]
    rows = helds[0].shape[1]
    scale = HEAD_DIM**-0.5 * LOG2E
    lane = lax.broadcasted_iota(jnp.int32, (rows, HEAD_DIM), 1)
    parts = [slice(j * span, (j + 1) * span) for j in range(rows // span)]
    for h, held_ref in enumerate(helds):
        wide = values.at[h % 2]
        wide[:, :HEAD_DIM] = held_ref[2]
        wide[:, HEAD_DIM:] = jnp.where(lane < 3, -1.0, 0.0).astype(BF16)
        for step in range(rows // block):
            here = slice(step * block, (step + 1) * block)
            query = held_ref[0, here]
            scores = [dot(query, held_ref[1, p], NT) for p in parts]
            peak = functools.reduce(
                jnp.maximum, [jnp.max(s, axis=-1, keepdims=True) for s in scores]
            )
            peak = peak * scale
            mixed = 0.0
            for p, one_scores in zip(parts, scores):
                raised = jnp.exp2(one_scores * scale - peak).astype(BF16)
                raised_ref[h, here, p] = raised
                mixed = mixed + dot(raised, wide[p])
            first_ref[h, here, :HEAD_DIM] = mixed[:, :HEAD_DIM]
            first_ref[h, here, HEAD_DIM:] = jnp.where(
                lane[:block] == 1, peak, mixed[:, HEAD_DIM:]
            )


def own_attention(helds, block=512, span=512):
    heads, rows = len(helds), helds[0].shape[1]
    return on_chip(
        functools.partial(own_kernel, heads, block, span),
        helds,
        [((heads, rows, rows), BF16), ((heads, rows, 2 * HEAD_DIM), F32)],
        [pltpu.VMEM((2, rows, 2 * HEAD_DIM), BF16)],
        us=11,
        name="own_attention",
    )


def far_kernel(heads, block, span, bias_ref, *refs):
    helds, refs = refs[:heads], refs[heads:]
    far_refs, raised_refs, (out_ref, part_ref, rest_ref, low_ref, high_ref) = (
        refs[:2], refs[2:4], refs[4:9],
    )
    for h in range(heads):
        far_head(
            h, heads, block, span, bias_ref, helds[h], *far_refs, *raised_refs, out_ref, part_ref,
            rest_ref, low_ref, high_ref, *(pair.at[h % 2] for pair in refs[9:]),
        )


def with_dots(grad, dots, lane):
    dots_a = dots.astype(BF16)
    dots = dots - dots_a.astype(F32)
    dots_b = dots.astype(BF16)
    dots_c = (dots - dots_b.astype(F32)).astype(BF16)
    zero = jnp.zeros_like(dots_c)
    tail = jnp.where(
        lane == 0, dots_a, jnp.where(lane == 1, dots_b, jnp.where(lane == 2, dots_c, zero))
    )
    return jnp.concatenate([grad, tail], 1)


def back_block(step, parts, weights, query, grad, grad_wide, factors, keys, values, dk_sum, dv_sum):
    query_turned = (query.astype(F32) * factors).astype(BF16).T
    grad_turned = (grad.astype(F32) * factors).astype(BF16).T
    query_grad = 0.0
    for p, one_weights in zip(parts, weights):
        prob_grads = dot(grad_wide, values[p], NT)
        score_grads = (one_weights.astype(F32) * prob_grads).astype(BF16)
        query_grad = query_grad + dot(score_grads, keys[p, :HEAD_DIM])
        key_part = dot(query_turned, score_grads)
        value_part = dot(grad_turned, one_weights)
        if step == 0:
            dk_sum[:, p] = key_part
            dv_sum[:, p] = value_part
        else:
            dk_sum[:, p] += key_part
            dv_sum[:, p] += value_part
    return query_grad * (factors * HEAD_DIM**-0.5)


def far_head(
    h, heads, block, span, bias_ref, held_ref, same_ref, cross_ref, first_ref, all_grads, out_ref,
    part_ref, rest_ref, low_ref, high_ref, keys, values, dk_sum, dv_sum, kept,
):
    rows = held_ref.shape[1]
    half = rows // 2
    head = slice(h * HEAD_DIM, (h + 1) * HEAD_DIM)
    factor = HEAD_DIM**-0.5
    scale = factor * LOG2E
    lane = lax.broadcasted_iota(jnp.int32, (rows, HEAD_DIM), 1)
    for i, far_ref in enumerate((same_ref, cross_ref)):
        there = slice(i * half, (i + 1) * half)
        keys[there] = far_ref[h]
        values[there, :HEAD_DIM] = far_ref[heads + h]
    values[:, HEAD_DIM:] = jnp.where(lane < 3, -1.0, 0.0).astype(BF16)
    lane = lane[:block]
    later = []
    parts = [slice(j * span, (j + 1) * span) for j in range(rows // span)]
    for step in range(rows // block):
        here = slice(step * block, (step + 1) * block)
        query = held_ref[0, here]
        scores = [dot(query, keys[p], NT) + bias_ref[j * span // half] for j, p in enumerate(parts)]
        begun = first_ref[h, here]
        own_peak = begun[:, HEAD_DIM + 1 : HEAD_DIM + 2]
        peak = functools.reduce(jnp.maximum, [jnp.max(s, axis=-1, keepdims=True) for s in scores])
        peak = jnp.maximum(peak * scale, own_peak)
        drop = jnp.exp2(own_peak - peak)
        mixed = begun * drop
        for p, one_scores in zip(parts, scores):
            raised = jnp.exp2(one_scores * scale - peak).astype(BF16)
            kept[here, p] = raised
            mixed = mixed + dot(raised, values[p])
        inverse = -1.0 / mixed[:, HEAD_DIM : HEAD_DIM + 1]
        grad = all_grads[here, head]
        attended = (mixed[:, :HEAD_DIM] * inverse).astype(BF16)
        out_ref[here, head] = attended
        dots = jnp.sum(grad.astype(F32) * attended.astype(F32), axis=-1, keepdims=True)
        rest_ref[h, here] = jnp.where(lane == 0, inverse * drop, dots)
        later.append((here, query, grad, dots, inverse))
    for step, (here, query, grad, dots, inverse) in enumerate(later):
        part_ref[here, head] = back_block(
            step, parts, [kept[here, p] for p in parts], query, grad, with_dots(grad, dots, lane), inverse, keys, values,
            dk_sum, dv_sum,
        )
    for out, first in ((low_ref, 0), (high_ref, half)):
        out[h] = (dk_sum[:, first : first + half].T * factor).astype(BF16)
        out[heads + h] = dv_sum[:, first : first + half].T.astype(BF16)


def back_kernel(heads, block, span, *refs):
    helds, refs = refs[:heads], refs[heads:]
    raw_ref, raised_ref, part_ref, rest_ref, all_grads, gain_ref = refs[:6]
    gq_ref, dk_ref, dv_ref = refs[6:9]
    rows = raw_ref.shape[1]
    lane = lax.broadcasted_iota(jnp.int32, (rows, HEAD_DIM), 1)
    parts = [slice(j * span, (j + 1) * span) for j in range(rows // span)]
    for h, held_ref in enumerate(helds):
        head = slice(h * HEAD_DIM, (h + 1) * HEAD_DIM)
        values, dk_sum, dv_sum = (pair.at[h % 2] for pair in refs[9:])
        values[:, :HEAD_DIM] = held_ref[2]
        values[:, HEAD_DIM:] = jnp.where(lane < 3, -1.0, 0.0).astype(BF16)
        for step in range(rows // block):
            here = slice(step * block, (step + 1) * block)
            rest = rest_ref[h, here]
            grad = all_grads[here, head]
            grad_wide = with_dots(grad, rest[:, 1:2], lane[:block])
            total = part_ref[here, head] + back_block(
                step, parts, [raised_ref[h, here, p] for p in parts], held_ref[0, here], grad,
                grad_wide, rest[:, :1], held_ref.at[1], values, dk_sum, dv_sum,
            )
            gq_ref[here, head] = norm_back(raw_ref[h, here], gain_ref[0:1], total)
        dk_ref[:, head] = dk_sum[...].T * HEAD_DIM**-0.5
        dv_ref[:, head] = dv_sum[...].T


def norm_back(raw, gain, grad):
    inverse_rms = lax.rsqrt(jnp.mean(raw * raw, axis=-1, keepdims=True) + EPSILON)
    weighted = grad * gain
    unit = raw * inverse_rms
    inner = jnp.mean(unit * weighted, axis=-1, keepdims=True)
    return (inverse_rms * (weighted - unit * inner)).astype(BF16)


def far_attention(bias, helds, far, first, out_grad, block=256, span=512):
    heads, rows = len(helds), helds[0].shape[1]
    width = heads * HEAD_DIM
    return on_chip(
        functools.partial(far_kernel, heads, block, span),
        [(bias, pltpu.SMEM), *helds, *far, first, out_grad],
        [((rows, width), BF16), ((rows, width), F32), ((heads, rows, HEAD_DIM), F32)]
        + [((2 * heads, rows // 2, HEAD_DIM), BF16)] * 2,
        [pltpu.VMEM((2, rows, HEAD_DIM), BF16), pltpu.VMEM((2, rows, 2 * HEAD_DIM), BF16)]
        + [pltpu.VMEM((2, HEAD_DIM, rows), F32)] * 2
        + [pltpu.VMEM((2, rows, rows), BF16)],
        us=15,
        name="far_attention",
    )


def back_attention(helds, raw, raised, part, rest, out_grad, gain, block=512, span=512):
    heads, rows = len(helds), helds[0].shape[1]
    width = heads * HEAD_DIM
    return on_chip(
        functools.partial(back_kernel, heads, block, span),
        [*helds, raw, raised, part, rest, out_grad, gain],
        [((rows, width), BF16)] + [((rows, width), F32)] * 2,
        [pltpu.VMEM((2, rows, 2 * HEAD_DIM), BF16)] + [pltpu.VMEM((2, HEAD_DIM, rows), F32)] * 2,
        us=13,
        name="back_attention",
    )


def split_rows(count, place_ref, straight, g, pieces, mine_ref, theirs_ref):
    chunk = straight.shape[0] // count
    for i in range(count):
        there = pl.ds(pl.multiple_of(place_ref[FIRST + i] * chunk, chunk), chunk)
        g[i * chunk : (i + 1) * chunk] = straight[there]
    blocks, rows, _ = mine_ref.shape
    low = place_ref[2] == 0
    for b in range(blocks):
        columns = slice(2 * b * rows, 2 * (b + 1) * rows)
        x = jnp.concatenate([piece[:, columns] for piece in pieces], 0)
        product = dot(x, g[...], TN).astype(BF16)
        mine_ref[b] = jnp.where(low, product[:rows], product[rows:])
        theirs_ref[b] = jnp.where(low, product[rows:], product[:rows])


def query_kernel(count, place_ref, gq_ref, *refs):
    mine_ref, theirs_ref, g = refs[-3:]
    split_rows(count, place_ref, gq_ref, g, refs[:-3], mine_ref, theirs_ref)


def key_value_kernel(
    count, heads, place_ref, dk_ref, dv_ref, same_ref, cross_ref, raw_ref, gain_ref, after_ref, *refs
):
    mine_ref, theirs_ref, straight, g = refs[-4:]
    half = dk_ref.shape[0] // 2
    for i, came in enumerate((same_ref, cross_ref)):
        mine = place_ref[3] if i == 0 else 1 - place_ref[3]
        rows = pl.ds(pl.multiple_of(mine * half, half), half)
        for h in range(heads):
            head = slice(h * HEAD_DIM, (h + 1) * HEAD_DIM)
            there = slice((heads + h) * HEAD_DIM, (heads + h + 1) * HEAD_DIM)
            dk = dk_ref[rows, head] + came[h].astype(F32)
            dv = dv_ref[rows, head] + came[heads + h].astype(F32)
            straight[rows, head] = norm_back(raw_ref[heads + h, rows], gain_ref[1:2], dk)
            straight[rows, there] = dv.astype(BF16)
    split_rows(count, place_ref, straight, g, refs[:-4], mine_ref, theirs_ref)


def weight_rows(kernel, groups, place, ins, total, width, held, us, name):
    pieces = [piece for group in groups for piece in group]
    out = ((8, pieces[0].shape[1] // 16, width), BF16)
    return on_chip(
        kernel,
        [(place, pltpu.SMEM), *ins, *pieces],
        [out, out],
        [pltpu.VMEM((total, width), BF16)] * held,
        us=us,
        name=name,
    )


def pair_kernel(place_ref, mine_q, came_q, mine_kv, came_kv, *outs):
    zh, x = place_ref[0], place_ref[1]
    rows = mine_q.shape[1] // 2
    along_x, (stay, leave) = outs[:4], outs[4:]
    at = 0
    for mine, came in ((mine_q, came_q), (mine_kv, came_kv)):
        columns = slice(at, at + mine.shape[2])
        at += mine.shape[2]
        for dx in range(4):
            for dz in range(2):
                b = ((zh + dz) % 2) * 4 + (x + dx) % 4
                both = (mine[b].astype(F32) + came[b].astype(F32)).astype(BF16)
                along_x[dx][dz, :, columns] = both[:rows]
                (leave if dz else stay)[dx, :, columns] = both[rows:]


def after_x_kernel(a_ref, b_ref, c_ref, d_ref, keep_ref, send_ref):
    for i, out in enumerate((keep_ref, send_ref)):
        summed = a_ref[i].astype(F32) + b_ref[i].astype(F32)
        summed = summed + c_ref[i].astype(F32) + d_ref[i].astype(F32)
        out[...] = summed.astype(out.dtype)


def after_z_kernel(stay_ref, came_ref, *outs):
    for dx, out in enumerate(outs):
        out[...] = (stay_ref[dx].astype(F32) + came_ref[dx].astype(F32)).astype(out.dtype)


def last_kernel(keep_x, came_x, keep_z, a_ref, b_ref, c_ref, out):
    rows = keep_x.shape[0]
    top = keep_x[...] + came_x[...].astype(F32)
    bottom = keep_z[...] + a_ref[...].astype(F32)
    bottom = bottom + b_ref[...].astype(F32) + c_ref[...].astype(F32)
    width = out.shape[2]
    for kind in range(3):
        columns = slice(kind * width, (kind + 1) * width)
        out[kind, :rows] = top[:, columns]
        out[kind, rows:] = bottom[:, columns]


def halves_kernel(first_ref, last_ref, first_half, last_half):
    cut = first_half.shape[0]
    first_half[...] = first_ref[:cut]
    last_half[...] = last_ref[cut:]


def per_device(hidden, qkv_weight, norm_gain, out_grad):
    depth, kinds, local = qkv_weight.shape
    heads = local // HEAD_DIM
    chunk = hidden.shape[0]
    total = chunk * lax.axis_size("tensor")
    half = total // 2
    frame = lax.axis_index("frame").astype(jnp.int32)
    frames = lax.axis_size("frame")
    tensor = lax.axis_index("tensor").astype(jnp.int32)
    zh, x, core = frame // 8, (frame // 2) % 4, frame % 2
    y, zl = tensor // 2, tensor % 2
    def at(dy, dz):
        return ((y + dy) % 4) * 2 + (zl + dz) % 2

    weight = qkv_weight.transpose(1, 0, 2)

    send = lambda value, dy, dz: lax.ppermute(value, "tensor", tensor_pairs(dy, dz))
    cut = chunk // 2
    below = send(hidden, 1, 0)
    above = send(hidden, -1, 0)
    side = send(hidden, 0, 1)
    far = send(above, -1, 0)
    side_above = send(above, 0, 1)
    side_below = send(side, 1, 0)
    first_half, last_half = on_chip(
        halves_kernel, [side_above, far], [((cut, depth), BF16)] * 2, name="halves"
    )
    side_far = (send(first_half, -1, 0), send(last_half, 0, 1))
    groups = [(hidden,), (below,), (above,), (side,), (far,), (side_below,), (side_above,), side_far]
    moves = [(0, 0), (-1, 0), (1, 0), (0, 1), (2, 0), (-1, 1), (1, 1), (2, 1)]
    mine = y // 2
    place = jnp.stack([zh, x, core, mine] + [at(*move) for move in moves])

    def proj(first, last, before, extra, us):
        return project(
            place, first, groups[first:last], weight, norm_gain, heads, total, before, extra, us
        )

    move = lambda value, pairs: lax.ppermute(value, ("frame", "tensor"), pairs)
    state = proj(0, 4, None, 0, 6)
    state = proj(4, 7, state, 0, 5)
    raw, *held, same, cross = proj(7, 8, state, 2, 2)
    far = (move(same, half_pairs(1)), move(cross, half_pairs(-1)))
    turn = 2 * mine - 1
    seen = lambda f: jnp.where((f >= 0) & (f < frames), 0.0, -1e30).astype(F32)
    bias = jnp.stack([seen(frame - turn), seen(frame + turn)])

    raised, first = own_attention(held)
    attended, part, rest, low, high = far_attention(bias, held, far, first, out_grad)
    gq, dk, dv = back_attention(held, raw, raised, part, rest, out_grad, norm_gain)
    same = move(low, [pair[::-1] for pair in half_pairs(1)])
    cross = move(high, [pair[::-1] for pair in half_pairs(-1)])
    count = len(groups)
    swap = lambda value: lax.ppermute(value, "frame", frame_pairs(0, 0, 1))
    mine_q, theirs_q = weight_rows(
        functools.partial(query_kernel, count), groups, place, [gq], total, local, 1, 5, "query"
    )
    mine_kv, theirs_kv = weight_rows(
        functools.partial(key_value_kernel, count, heads),
        groups,
        place,
        [dk, dv, same, cross, raw, norm_gain, (mine_q, pl.ANY)],
        total,
        2 * local,
        2,
        8,
        "key_value",
    )
    rows = mine_q.shape[1] // 2
    wide = kinds * local
    piece = ((2, rows, wide), BF16)
    line = ((4, rows, wide), BF16)
    *along_x, stay, leave = on_chip(
        pair_kernel,
        [(place, pltpu.SMEM), mine_q, swap(theirs_q), mine_kv, swap(theirs_kv)],
        [piece] * 4 + [line] * 2,
        name="pair",
    )
    shift = lambda value, dx, dz: lax.ppermute(value, "frame", frame_pairs(dx, dz))
    came = shift(leave, 0, 1)
    moved = [shift(along_x[dx], dx, 0) for dx in (1, 3, 2)]
    one = (rows, wide)
    keep_x, send_x = on_chip(
        after_x_kernel, [along_x[0], *moved], [(one, F32), (one, BF16)], name="after_x"
    )
    came_x = shift(send_x, 0, 1)
    keep_z, *send_z = on_chip(
        after_z_kernel, [stay, came], [(one, F32)] + [(one, BF16)] * 3, name="after_z"
    )
    came_z = [shift(send_z[dx - 1], dx, 0) for dx in (1, 3, 2)]
    (weight_grad,) = on_chip(
        last_kernel,
        [keep_x, came_x, keep_z, *came_z],
        [((kinds, 2 * rows, local), F32)],
        name="last",
    )
    return (attended, weight_grad.transpose(1, 0, 2))


def solution(mesh):
    placed = (P(("frame", "tensor"), None), P(None, None, "tensor"), P(), P("frame", "tensor"))
    return jax.shard_map(
        per_device,
        mesh=mesh,
        in_specs=placed,
        out_specs=(P("frame", "tensor"), P("frame", None, "tensor")),
        check_vma=False,
    )
```

```python
import functools

import jax
import jax.numpy as jnp
from jax import lax
from jax.experimental import pallas as pl
from jax.experimental.pallas import tpu as pltpu
from jax.sharding import PartitionSpec as P

HEAD_DIM = 128
EPSILON = 1e-06
LOG2E = 1.4426950408889634
LIMIT = 24
FIRST = 4
F32 = jnp.float32
BF16 = jnp.bfloat16
NN = (((1,), (0,)), ((), ()))
NT = (((1,), (1,)), ((), ()))
TN = (((0,), (0,)), ((), ()))


def dot(left, right, dims=NN):
    return lax.dot_general(left, right, dims, preferred_element_type=F32)


def on_chip(kernel, ins, outs, scratch=(), limit=LIMIT, aliases=None, us=0.1, name=None):
    specs, args = [], []
    for one in ins:
        space = pltpu.VMEM
        if isinstance(one, tuple):
            one, space = one
        specs.append(pl.BlockSpec(memory_space=space))
        args.append(one)
    return pl.pallas_call(
        kernel,
        in_specs=specs,
        out_specs=[pl.BlockSpec(memory_space=(out + (pltpu.VMEM,))[2]) for out in outs],
        out_shape=[jax.ShapeDtypeStruct(*out[:2]) for out in outs],
        scratch_shapes=list(scratch),
        input_output_aliases=aliases or {},
        compiler_params=pltpu.CompilerParams(vmem_limit_bytes=limit * 1024 * 1024),
        cost_estimate=pl.CostEstimate(
            flops=int(us * 1.1e9), bytes_accessed=0, transcendentals=0
        ),
        name=name,
    )(*args)


def frame_pairs(dx, dz, dc=0):
    return [
        (zh * 8 + x * 2 + c, ((zh + dz) % 2) * 8 + ((x + dx) % 4) * 2 + (c + dc) % 2)
        for zh in range(2)
        for x in range(4)
        for c in range(2)
    ]


def tensor_pairs(dy, dz):
    return [
        (y * 2 + z, ((y + dy) % 4) * 2 + (z + dz) % 2) for y in range(4) for z in range(2)
    ]


def half_pairs(sign):
    pairs = []
    for f in range(16):
        for t in range(8):
            there = f + (sign if t // 4 else -sign)
            if 0 <= there < 16:
                pairs.append((f * 8 + t, there * 8 + t))
    return pairs


def proj_kernel(heads, groups, first, extra, place_ref, gain_ref, w_ref, *refs):
    raw_ref, *outs, x_ref = refs[sum(groups) + (1 + heads) * (first > FIRST) :]
    held, sent = outs[:heads], outs[heads:]
    at = 0
    for ref in refs[: sum(groups)]:
        x_ref[at : at + ref.shape[0]] = ref[...]
        at += ref.shape[0]
    rows = at // len(groups)
    for kind in (1, 2, 0):
        projected = dot(x_ref[...], w_ref[kind])
        for h in range(heads):
            part = projected[:, h * HEAD_DIM : (h + 1) * HEAD_DIM]
            rounded = part.astype(BF16) if kind == 2 else normed(part, gain_ref[kind : kind + 1])
            for i in range(len(groups)):
                there = pl.ds(pl.multiple_of(place_ref[first + i] * rows, rows), rows)
                here = slice(i * rows, (i + 1) * rows)
                held[h][kind, there] = rounded[here]
                if kind < 2:
                    raw_ref[kind * heads + h, there] = part[here]
    if extra:
        half = raw_ref.shape[1] // 2
        for i, out in enumerate(sent):
            mine = place_ref[3] if i == 0 else 1 - place_ref[3]
            there = pl.ds(pl.multiple_of(mine * half, half), half)
            for h in range(heads):
                out[h] = held[h][1, there]
                out[heads + h] = held[h][2, there]


def normed(raw, gain):
    inverse_rms = lax.rsqrt(jnp.mean(raw * raw, axis=-1, keepdims=True) + EPSILON)
    return (raw * inverse_rms * gain).astype(BF16)


def project(place, first, groups, weight, gain, heads, total, before, extra, us):
    rows = sum(piece.shape[0] for piece in groups[0])
    depth = weight.shape[1]
    outs = [((2 * heads, total, HEAD_DIM), F32)] + [((3, total, HEAD_DIM), BF16)] * heads
    outs += [((2 * heads, total // 2, HEAD_DIM), BF16)] * extra
    ins = [(place, pltpu.SMEM), gain, weight] + [piece for group in groups for piece in group]
    aliases = {}
    if before is not None:
        aliases = {len(ins) + i: i for i in range(1 + heads)}
        ins += list(before)
    counts = tuple(len(group) for group in groups)
    return on_chip(
        functools.partial(proj_kernel, heads, counts, FIRST + first, extra),
        ins,
        outs,
        [pltpu.VMEM((rows * len(groups), depth), BF16)],
        aliases=aliases,
        us=us,
        name="project",
    )


def own_kernel(heads, block, span, *refs):
    helds, (raised_ref, first_ref, values) = refs[:heads], refs[heads:]
    rows = helds[0].shape[1]
    scale = HEAD_DIM**-0.5 * LOG2E
    lane = lax.broadcasted_iota(jnp.int32, (rows, HEAD_DIM), 1)
    parts = [slice(j * span, (j + 1) * span) for j in range(rows // span)]
    for h, held_ref in enumerate(helds):
        wide = values.at[h % 2]
        wide[:, :HEAD_DIM] = held_ref[2]
        wide[:, HEAD_DIM:] = jnp.where(lane < 3, -1.0, 0.0).astype(BF16)
        for step in range(rows // block):
            here = slice(step * block, (step + 1) * block)
            query = held_ref[0, here]
            scores = [dot(query, held_ref[1, p], NT) for p in parts]
            peak = functools.reduce(
                jnp.maximum, [jnp.max(s, axis=-1, keepdims=True) for s in scores]
            )
            peak = peak * scale
            mixed = 0.0
            for p, one_scores in zip(parts, scores):
                raised = jnp.exp2(one_scores * scale - peak).astype(BF16)
                raised_ref[h, here, p] = raised
                mixed = mixed + dot(raised, wide[p])
            first_ref[h, here, :HEAD_DIM] = mixed[:, :HEAD_DIM]
            first_ref[h, here, HEAD_DIM:] = jnp.where(
                lane[:block] == 1, peak, mixed[:, HEAD_DIM:]
            )


def own_attention(helds, block=512, span=512):
    heads, rows = len(helds), helds[0].shape[1]
    return on_chip(
        functools.partial(own_kernel, heads, block, span),
        helds,
        [((heads, rows, rows), BF16), ((heads, rows, 2 * HEAD_DIM), F32)],
        [pltpu.VMEM((2, rows, 2 * HEAD_DIM), BF16)],
        us=11,
        name="own_attention",
    )


def far_kernel(heads, block, span, bias_ref, *refs):
    helds, refs = refs[:heads], refs[heads:]
    far_refs, raised_refs, (out_ref, part_ref, rest_ref, low_ref, high_ref) = (
        refs[:2], refs[2:4], refs[4:9],
    )
    for h in range(heads):
        far_head(
            h, heads, block, span, bias_ref, helds[h], *far_refs, *raised_refs, out_ref, part_ref,
            rest_ref, low_ref, high_ref, *(pair.at[h % 2] for pair in refs[9:]),
        )


def with_dots(grad, dots, lane):
    dots_a = dots.astype(BF16)
    dots = dots - dots_a.astype(F32)
    dots_b = dots.astype(BF16)
    dots_c = (dots - dots_b.astype(F32)).astype(BF16)
    zero = jnp.zeros_like(dots_c)
    tail = jnp.where(
        lane == 0, dots_a, jnp.where(lane == 1, dots_b, jnp.where(lane == 2, dots_c, zero))
    )
    return jnp.concatenate([grad, tail], 1)


def back_block(step, parts, weights, query, grad, grad_wide, factors, keys, values, dk_sum, dv_sum):
    query_turned = (query.astype(F32) * factors).astype(BF16).T
    grad_turned = (grad.astype(F32) * factors).astype(BF16).T
    query_grad = 0.0
    for p, one_weights in zip(parts, weights):
        prob_grads = dot(grad_wide, values[p], NT)
        score_grads = (one_weights.astype(F32) * prob_grads).astype(BF16)
        query_grad = query_grad + dot(score_grads, keys[p, :HEAD_DIM])
        key_part = dot(query_turned, score_grads)
        value_part = dot(grad_turned, one_weights)
        if step == 0:
            dk_sum[:, p] = key_part
            dv_sum[:, p] = value_part
        else:
            dk_sum[:, p] += key_part
            dv_sum[:, p] += value_part
    return query_grad * (factors * HEAD_DIM**-0.5)


def far_head(
    h, heads, block, span, bias_ref, held_ref, same_ref, cross_ref, first_ref, all_grads, out_ref,
    part_ref, rest_ref, low_ref, high_ref, keys, values, dk_sum, dv_sum, kept,
):
    rows = held_ref.shape[1]
    half = rows // 2
    head = slice(h * HEAD_DIM, (h + 1) * HEAD_DIM)
    factor = HEAD_DIM**-0.5
    scale = factor * LOG2E
    lane = lax.broadcasted_iota(jnp.int32, (rows, HEAD_DIM), 1)
    for i, far_ref in enumerate((same_ref, cross_ref)):
        there = slice(i * half, (i + 1) * half)
        keys[there] = far_ref[h]
        values[there, :HEAD_DIM] = far_ref[heads + h]
    values[:, HEAD_DIM:] = jnp.where(lane < 3, -1.0, 0.0).astype(BF16)
    lane = lane[:block]
    later = []
    parts = [slice(j * span, (j + 1) * span) for j in range(rows // span)]
    for step in range(rows // block):
        here = slice(step * block, (step + 1) * block)
        query = held_ref[0, here]
        scores = [dot(query, keys[p], NT) + bias_ref[j * span // half] for j, p in enumerate(parts)]
        begun = first_ref[h, here]
        own_peak = begun[:, HEAD_DIM + 1 : HEAD_DIM + 2]
        peak = functools.reduce(jnp.maximum, [jnp.max(s, axis=-1, keepdims=True) for s in scores])
        peak = jnp.maximum(peak * scale, own_peak)
        drop = jnp.exp2(own_peak - peak)
        mixed = begun * drop
        for p, one_scores in zip(parts, scores):
            raised = jnp.exp2(one_scores * scale - peak).astype(BF16)
            kept[here, p] = raised
            mixed = mixed + dot(raised, values[p])
        inverse = -1.0 / mixed[:, HEAD_DIM : HEAD_DIM + 1]
        grad = all_grads[here, head]
        attended = (mixed[:, :HEAD_DIM] * inverse).astype(BF16)
        out_ref[here, head] = attended
        dots = jnp.sum(grad.astype(F32) * attended.astype(F32), axis=-1, keepdims=True)
        rest_ref[h, here] = jnp.where(lane == 0, inverse * drop, dots)
        later.append((here, query, grad, dots, inverse))
    for step, (here, query, grad, dots, inverse) in enumerate(later):
        part_ref[here, head] = back_block(
            step, parts, [kept[here, p] for p in parts], query, grad, with_dots(grad, dots, lane), inverse, keys, values,
            dk_sum, dv_sum,
        )
    for out, first in ((low_ref, 0), (high_ref, half)):
        out[h] = (dk_sum[:, first : first + half].T * factor).astype(BF16)
        out[heads + h] = dv_sum[:, first : first + half].T.astype(BF16)


def back_kernel(heads, block, span, *refs):
    helds, refs = refs[:heads], refs[heads:]
    raw_ref, raised_ref, part_ref, rest_ref, all_grads, gain_ref = refs[:6]
    gq_ref, dk_ref, dv_ref = refs[6:9]
    rows = raw_ref.shape[1]
    lane = lax.broadcasted_iota(jnp.int32, (rows, HEAD_DIM), 1)
    parts = [slice(j * span, (j + 1) * span) for j in range(rows // span)]
    for h, held_ref in enumerate(helds):
        head = slice(h * HEAD_DIM, (h + 1) * HEAD_DIM)
        values, dk_sum, dv_sum = (pair.at[h % 2] for pair in refs[9:])
        values[:, :HEAD_DIM] = held_ref[2]
        values[:, HEAD_DIM:] = jnp.where(lane < 3, -1.0, 0.0).astype(BF16)
        for step in range(rows // block):
            here = slice(step * block, (step + 1) * block)
            rest = rest_ref[h, here]
            grad = all_grads[here, head]
            grad_wide = with_dots(grad, rest[:, 1:2], lane[:block])
            total = part_ref[here, head] + back_block(
                step, parts, [raised_ref[h, here, p] for p in parts], held_ref[0, here], grad,
                grad_wide, rest[:, :1], held_ref.at[1], values, dk_sum, dv_sum,
            )
            gq_ref[here, head] = norm_back(raw_ref[h, here], gain_ref[0:1], total)
        dk_ref[:, head] = dk_sum[...].T * HEAD_DIM**-0.5
        dv_ref[:, head] = dv_sum[...].T


def norm_back(raw, gain, grad):
    inverse_rms = lax.rsqrt(jnp.mean(raw * raw, axis=-1, keepdims=True) + EPSILON)
    weighted = grad * gain
    unit = raw * inverse_rms
    inner = jnp.mean(unit * weighted, axis=-1, keepdims=True)
    return (inverse_rms * (weighted - unit * inner)).astype(BF16)


def far_attention(bias, helds, far, first, out_grad, block=256, span=512):
    heads, rows = len(helds), helds[0].shape[1]
    width = heads * HEAD_DIM
    return on_chip(
        functools.partial(far_kernel, heads, block, span),
        [(bias, pltpu.SMEM), *helds, *far, first, out_grad],
        [((rows, width), BF16), ((rows, width), F32), ((heads, rows, HEAD_DIM), F32)]
        + [((2 * heads, rows // 2, HEAD_DIM), BF16)] * 2,
        [pltpu.VMEM((2, rows, HEAD_DIM), BF16), pltpu.VMEM((2, rows, 2 * HEAD_DIM), BF16)]
        + [pltpu.VMEM((2, HEAD_DIM, rows), F32)] * 2
        + [pltpu.VMEM((2, rows, rows), BF16)],
        us=15,
        name="far_attention",
    )


def back_attention(helds, raw, raised, part, rest, out_grad, gain, block=512, span=512):
    heads, rows = len(helds), helds[0].shape[1]
    width = heads * HEAD_DIM
    return on_chip(
        functools.partial(back_kernel, heads, block, span),
        [*helds, raw, raised, part, rest, out_grad, gain],
        [((rows, width), BF16)] + [((rows, width), F32)] * 2,
        [pltpu.VMEM((2, rows, 2 * HEAD_DIM), BF16)] + [pltpu.VMEM((2, HEAD_DIM, rows), F32)] * 2,
        us=13,
        name="back_attention",
    )


def split_rows(count, place_ref, straight, g, pieces, mine_ref, theirs_ref):
    chunk = straight.shape[0] // count
    for i in range(count):
        there = pl.ds(pl.multiple_of(place_ref[FIRST + i] * chunk, chunk), chunk)
        g[i * chunk : (i + 1) * chunk] = straight[there]
    blocks, rows, _ = mine_ref.shape
    low = place_ref[2] == 0
    for b in range(blocks):
        columns = slice(2 * b * rows, 2 * (b + 1) * rows)
        x = jnp.concatenate([piece[:, columns] for piece in pieces], 0)
        product = dot(x, g[...], TN).astype(BF16)
        mine_ref[b] = jnp.where(low, product[:rows], product[rows:])
        theirs_ref[b] = jnp.where(low, product[rows:], product[:rows])


def query_kernel(count, place_ref, gq_ref, *refs):
    mine_ref, theirs_ref, g = refs[-3:]
    split_rows(count, place_ref, gq_ref, g, refs[:-3], mine_ref, theirs_ref)


def key_value_kernel(
    count, heads, place_ref, dk_ref, dv_ref, same_ref, cross_ref, raw_ref, gain_ref, after_ref, *refs
):
    mine_ref, theirs_ref, straight, g = refs[-4:]
    half = dk_ref.shape[0] // 2
    for i, came in enumerate((same_ref, cross_ref)):
        mine = place_ref[3] if i == 0 else 1 - place_ref[3]
        rows = pl.ds(pl.multiple_of(mine * half, half), half)
        for h in range(heads):
            head = slice(h * HEAD_DIM, (h + 1) * HEAD_DIM)
            there = slice((heads + h) * HEAD_DIM, (heads + h + 1) * HEAD_DIM)
            dk = dk_ref[rows, head] + came[h].astype(F32)
            dv = dv_ref[rows, head] + came[heads + h].astype(F32)
            straight[rows, head] = norm_back(raw_ref[heads + h, rows], gain_ref[1:2], dk)
            straight[rows, there] = dv.astype(BF16)
    split_rows(count, place_ref, straight, g, refs[:-4], mine_ref, theirs_ref)


def weight_rows(kernel, groups, place, ins, total, width, held, us, name):
    pieces = [piece for group in groups for piece in group]
    out = ((8, pieces[0].shape[1] // 16, width), BF16)
    return on_chip(
        kernel,
        [(place, pltpu.SMEM), *ins, *pieces],
        [out, out],
        [pltpu.VMEM((total, width), BF16)] * held,
        us=us,
        name=name,
    )


def pair_kernel(place_ref, mine_q, came_q, mine_kv, came_kv, *outs):
    zh, x = place_ref[0], place_ref[1]
    rows = mine_q.shape[1] // 2
    along_x, (stay, leave) = outs[:4], outs[4:]
    at = 0
    for mine, came in ((mine_q, came_q), (mine_kv, came_kv)):
        columns = slice(at, at + mine.shape[2])
        at += mine.shape[2]
        for dx in range(4):
            for dz in range(2):
                b = ((zh + dz) % 2) * 4 + (x + dx) % 4
                both = (mine[b].astype(F32) + came[b].astype(F32)).astype(BF16)
                along_x[dx][dz, :, columns] = both[:rows]
                (leave if dz else stay)[dx, :, columns] = both[rows:]


def after_x_kernel(a_ref, b_ref, c_ref, d_ref, keep_ref, send_ref):
    for i, out in enumerate((keep_ref, send_ref)):
        summed = a_ref[i].astype(F32) + b_ref[i].astype(F32)
        summed = summed + c_ref[i].astype(F32) + d_ref[i].astype(F32)
        out[...] = summed.astype(out.dtype)


def after_z_kernel(stay_ref, came_ref, *outs):
    for dx, out in enumerate(outs):
        out[...] = (stay_ref[dx].astype(F32) + came_ref[dx].astype(F32)).astype(out.dtype)


def last_kernel(keep_x, came_x, keep_z, a_ref, b_ref, c_ref, out):
    rows = keep_x.shape[0]
    top = keep_x[...] + came_x[...].astype(F32)
    bottom = keep_z[...] + a_ref[...].astype(F32)
    bottom = bottom + b_ref[...].astype(F32) + c_ref[...].astype(F32)
    width = out.shape[2]
    for kind in range(3):
        columns = slice(kind * width, (kind + 1) * width)
        out[kind, :rows] = top[:, columns]
        out[kind, rows:] = bottom[:, columns]


def halves_kernel(first_ref, last_ref, first_half, last_half):
    cut = first_half.shape[0]
    first_half[...] = first_ref[:cut]
    last_half[...] = last_ref[cut:]


def per_device(hidden, qkv_weight, norm_gain, out_grad):
    depth, kinds, local = qkv_weight.shape
    heads = local // HEAD_DIM
    chunk = hidden.shape[0]
    total = chunk * lax.axis_size("tensor")
    half = total // 2
    frame = lax.axis_index("frame").astype(jnp.int32)
    frames = lax.axis_size("frame")
    tensor = lax.axis_index("tensor").astype(jnp.int32)
    zh, x, core = frame // 8, (frame // 2) % 4, frame % 2
    y, zl = tensor // 2, tensor % 2
    def at(dy, dz):
        return ((y + dy) % 4) * 2 + (zl + dz) % 2

    weight = qkv_weight.transpose(1, 0, 2)

    send = lambda value, dy, dz: lax.ppermute(value, "tensor", tensor_pairs(dy, dz))
    cut = chunk // 2
    below = send(hidden, 1, 0)
    above = send(hidden, -1, 0)
    side = send(hidden, 0, 1)
    far = send(above, -1, 0)
    side_above = send(above, 0, 1)
    side_below = send(side, 1, 0)
    first_half, last_half = on_chip(
        halves_kernel, [side_above, far], [((cut, depth), BF16)] * 2, name="halves"
    )
    side_far = (send(first_half, -1, 0), send(last_half, 0, 1))
    groups = [(hidden,), (below,), (above,), (side,), (far,), (side_below,), (side_above,), side_far]
    moves = [(0, 0), (-1, 0), (1, 0), (0, 1), (2, 0), (-1, 1), (1, 1), (2, 1)]
    mine = y // 2
    place = jnp.stack([zh, x, core, mine] + [at(*move) for move in moves])

    def proj(first, last, before, extra, us):
        return project(
            place, first, groups[first:last], weight, norm_gain, heads, total, before, extra, us
        )

    move = lambda value, pairs: lax.ppermute(value, ("frame", "tensor"), pairs)
    state = proj(0, 4, None, 0, 6)
    state = proj(4, 7, state, 0, 5)
    raw, *held, same, cross = proj(7, 8, state, 2, 2)
    far = (move(same, half_pairs(1)), move(cross, half_pairs(-1)))
    turn = 2 * mine - 1
    seen = lambda f: jnp.where((f >= 0) & (f < frames), 0.0, -1e30).astype(F32)
    bias = jnp.stack([seen(frame - turn), seen(frame + turn)])

    raised, first = own_attention(held)
    attended, part, rest, low, high = far_attention(bias, held, far, first, out_grad)
    gq, dk, dv = back_attention(held, raw, raised, part, rest, out_grad, norm_gain)
    same = move(low, [pair[::-1] for pair in half_pairs(1)])
    cross = move(high, [pair[::-1] for pair in half_pairs(-1)])
    count = len(groups)
    swap = lambda value: lax.ppermute(value, "frame", frame_pairs(0, 0, 1))
    mine_q, theirs_q = weight_rows(
        functools.partial(query_kernel, count), groups, place, [gq], total, local, 1, 5, "query"
    )
    mine_kv, theirs_kv = weight_rows(
        functools.partial(key_value_kernel, count, heads),
        groups,
        place,
        [dk, dv, same, cross, raw, norm_gain, (mine_q, pl.ANY)],
        total,
        2 * local,
        2,
        8,
        "key_value",
    )
    rows = mine_q.shape[1] // 2
    wide = kinds * local
    piece = ((2, rows, wide), BF16)
    line = ((4, rows, wide), BF16)
    *along_x, stay, leave = on_chip(
        pair_kernel,
        [(place, pltpu.SMEM), mine_q, swap(theirs_q), mine_kv, swap(theirs_kv)],
        [piece] * 4 + [line] * 2,
        name="pair",
    )
    shift = lambda value, dx, dz: lax.ppermute(value, "frame", frame_pairs(dx, dz))
    came = shift(leave, 0, 1)
    moved = [shift(along_x[dx], dx, 0) for dx in (2, 1, 3)]
    one = (rows, wide)
    keep_x, send_x = on_chip(
        after_x_kernel, [along_x[0], *moved], [(one, F32), (one, BF16)], name="after_x"
    )
    came_x = shift(send_x, 0, 1)
    keep_z, *send_z = on_chip(
        after_z_kernel, [stay, came], [(one, F32)] + [(one, BF16)] * 3, name="after_z"
    )
    came_z = [shift(send_z[dx - 1], dx, 0) for dx in (2, 1, 3)]
    (weight_grad,) = on_chip(
        last_kernel,
        [keep_x, came_x, keep_z, *came_z],
        [((kinds, 2 * rows, local), F32)],
        name="last",
    )
    return (attended, weight_grad.transpose(1, 0, 2))


def solution(mesh):
    placed = (P(("frame", "tensor"), None), P(None, None, "tensor"), P(), P("frame", "tensor"))
    return jax.shard_map(
        per_device,
        mesh=mesh,
        in_specs=placed,
        out_specs=(P("frame", "tensor"), P("frame", None, "tensor")),
        check_vma=False,
    )
```

```python
import functools

import jax
import jax.numpy as jnp
from jax import lax
from jax.experimental import pallas as pl
from jax.experimental.pallas import tpu as pltpu
from jax.sharding import PartitionSpec as P

HEAD_DIM = 128
EPSILON = 1e-06
LOG2E = 1.4426950408889634
LIMIT = 24
FIRST = 4
F32 = jnp.float32
BF16 = jnp.bfloat16
NN = (((1,), (0,)), ((), ()))
NT = (((1,), (1,)), ((), ()))
TN = (((0,), (0,)), ((), ()))


def dot(left, right, dims=NN):
    return lax.dot_general(left, right, dims, preferred_element_type=F32)


def on_chip(kernel, ins, outs, scratch=(), limit=LIMIT, aliases=None, us=0.1, name=None):
    specs, args = [], []
    for one in ins:
        space = pltpu.VMEM
        if isinstance(one, tuple):
            one, space = one
        specs.append(pl.BlockSpec(memory_space=space))
        args.append(one)
    return pl.pallas_call(
        kernel,
        in_specs=specs,
        out_specs=[pl.BlockSpec(memory_space=(out + (pltpu.VMEM,))[2]) for out in outs],
        out_shape=[jax.ShapeDtypeStruct(*out[:2]) for out in outs],
        scratch_shapes=list(scratch),
        input_output_aliases=aliases or {},
        compiler_params=pltpu.CompilerParams(vmem_limit_bytes=limit * 1024 * 1024),
        cost_estimate=pl.CostEstimate(
            flops=int(us * 1.1e9), bytes_accessed=0, transcendentals=0
        ),
        name=name,
    )(*args)


def frame_pairs(dx, dz, dc=0):
    return [
        (zh * 8 + x * 2 + c, ((zh + dz) % 2) * 8 + ((x + dx) % 4) * 2 + (c + dc) % 2)
        for zh in range(2)
        for x in range(4)
        for c in range(2)
    ]


def tensor_pairs(dy, dz):
    return [
        (y * 2 + z, ((y + dy) % 4) * 2 + (z + dz) % 2) for y in range(4) for z in range(2)
    ]


def half_pairs(sign):
    pairs = []
    for f in range(16):
        for t in range(8):
            there = f + (sign if t // 4 else -sign)
            if 0 <= there < 16:
                pairs.append((f * 8 + t, there * 8 + t))
    return pairs


def proj_kernel(heads, groups, first, extra, place_ref, gain_ref, w_ref, *refs):
    raw_ref, *outs, x_ref = refs[sum(groups) + (1 + heads) * (first > FIRST) :]
    held, sent = outs[:heads], outs[heads:]
    at = 0
    for ref in refs[: sum(groups)]:
        x_ref[at : at + ref.shape[0]] = ref[...]
        at += ref.shape[0]
    rows = at // len(groups)
    for kind in (1, 2, 0):
        projected = dot(x_ref[...], w_ref[kind])
        for h in range(heads):
            part = projected[:, h * HEAD_DIM : (h + 1) * HEAD_DIM]
            rounded = part.astype(BF16) if kind == 2 else normed(part, gain_ref[kind : kind + 1])
            for i in range(len(groups)):
                there = pl.ds(pl.multiple_of(place_ref[first + i] * rows, rows), rows)
                here = slice(i * rows, (i + 1) * rows)
                held[h][kind, there] = rounded[here]
                if kind < 2:
                    raw_ref[kind * heads + h, there] = part[here]
    if extra:
        half = raw_ref.shape[1] // 2
        for i, out in enumerate(sent):
            mine = place_ref[3] if i == 0 else 1 - place_ref[3]
            there = pl.ds(pl.multiple_of(mine * half, half), half)
            for h in range(heads):
                out[h] = held[h][1, there]
                out[heads + h] = held[h][2, there]


def normed(raw, gain):
    inverse_rms = lax.rsqrt(jnp.mean(raw * raw, axis=-1, keepdims=True) + EPSILON)
    return (raw * inverse_rms * gain).astype(BF16)


def project(place, first, groups, weight, gain, heads, total, before, extra, us):
    rows = sum(piece.shape[0] for piece in groups[0])
    depth = weight.shape[1]
    outs = [((2 * heads, total, HEAD_DIM), F32)] + [((3, total, HEAD_DIM), BF16)] * heads
    outs += [((2 * heads, total // 2, HEAD_DIM), BF16)] * extra
    ins = [(place, pltpu.SMEM), gain, weight] + [piece for group in groups for piece in group]
    aliases = {}
    if before is not None:
        aliases = {len(ins) + i: i for i in range(1 + heads)}
        ins += list(before)
    counts = tuple(len(group) for group in groups)
    return on_chip(
        functools.partial(proj_kernel, heads, counts, FIRST + first, extra),
        ins,
        outs,
        [pltpu.VMEM((rows * len(groups), depth), BF16)],
        aliases=aliases,
        us=us,
        name="project",
    )


def own_kernel(heads, block, span, *refs):
    helds, (raised_ref, first_ref, values) = refs[:heads], refs[heads:]
    rows = helds[0].shape[1]
    scale = HEAD_DIM**-0.5 * LOG2E
    lane = lax.broadcasted_iota(jnp.int32, (rows, HEAD_DIM), 1)
    parts = [slice(j * span, (j + 1) * span) for j in range(rows // span)]
    for h, held_ref in enumerate(helds):
        wide = values.at[h % 2]
        wide[:, :HEAD_DIM] = held_ref[2]
        wide[:, HEAD_DIM:] = jnp.where(lane < 3, -1.0, 0.0).astype(BF16)
        for step in range(rows // block):
            here = slice(step * block, (step + 1) * block)
            query = held_ref[0, here]
            scores = [dot(query, held_ref[1, p], NT) for p in parts]
            peak = functools.reduce(
                jnp.maximum, [jnp.max(s, axis=-1, keepdims=True) for s in scores]
            )
            peak = peak * scale
            mixed = 0.0
            for p, one_scores in zip(parts, scores):
                raised = jnp.exp2(one_scores * scale - peak).astype(BF16)
                raised_ref[h, here, p] = raised
                mixed = mixed + dot(raised, wide[p])
            first_ref[h, here, :HEAD_DIM] = mixed[:, :HEAD_DIM]
            first_ref[h, here, HEAD_DIM:] = jnp.where(
                lane[:block] == 1, peak, mixed[:, HEAD_DIM:]
            )


def own_attention(helds, block=512, span=512):
    heads, rows = len(helds), helds[0].shape[1]
    return on_chip(
        functools.partial(own_kernel, heads, block, span),
        helds,
        [((heads, rows, rows), BF16), ((heads, rows, 2 * HEAD_DIM), F32)],
        [pltpu.VMEM((2, rows, 2 * HEAD_DIM), BF16)],
        us=11,
        name="own_attention",
    )


def far_kernel(heads, block, span, bias_ref, *refs):
    helds, refs = refs[:heads], refs[heads:]
    far_refs, raised_refs, (out_ref, part_ref, rest_ref, low_ref, high_ref) = (
        refs[:2], refs[2:4], refs[4:9],
    )
    for h in range(heads):
        far_head(
            h, heads, block, span, bias_ref, helds[h], *far_refs, *raised_refs, out_ref, part_ref,
            rest_ref, low_ref, high_ref, *(pair.at[h % 2] for pair in refs[9:]),
        )


def with_dots(grad, dots, lane):
    dots_a = dots.astype(BF16)
    dots = dots - dots_a.astype(F32)
    dots_b = dots.astype(BF16)
    dots_c = (dots - dots_b.astype(F32)).astype(BF16)
    zero = jnp.zeros_like(dots_c)
    tail = jnp.where(
        lane == 0, dots_a, jnp.where(lane == 1, dots_b, jnp.where(lane == 2, dots_c, zero))
    )
    return jnp.concatenate([grad, tail], 1)


def back_block(step, parts, weights, query, grad, grad_wide, factors, keys, values, dk_sum, dv_sum):
    query_turned = (query.astype(F32) * factors).astype(BF16).T
    grad_turned = (grad.astype(F32) * factors).astype(BF16).T
    query_grad = 0.0
    for p, one_weights in zip(parts, weights):
        prob_grads = dot(grad_wide, values[p], NT)
        score_grads = (one_weights.astype(F32) * prob_grads).astype(BF16)
        query_grad = query_grad + dot(score_grads, keys[p, :HEAD_DIM])
        key_part = dot(query_turned, score_grads)
        value_part = dot(grad_turned, one_weights)
        if step == 0:
            dk_sum[:, p] = key_part
            dv_sum[:, p] = value_part
        else:
            dk_sum[:, p] += key_part
            dv_sum[:, p] += value_part
    return query_grad * (factors * HEAD_DIM**-0.5)


def far_head(
    h, heads, block, span, bias_ref, held_ref, same_ref, cross_ref, first_ref, all_grads, out_ref,
    part_ref, rest_ref, low_ref, high_ref, keys, values, dk_sum, dv_sum, kept,
):
    rows = held_ref.shape[1]
    half = rows // 2
    head = slice(h * HEAD_DIM, (h + 1) * HEAD_DIM)
    factor = HEAD_DIM**-0.5
    scale = factor * LOG2E
    lane = lax.broadcasted_iota(jnp.int32, (rows, HEAD_DIM), 1)
    for i, far_ref in enumerate((same_ref, cross_ref)):
        there = slice(i * half, (i + 1) * half)
        keys[there] = far_ref[h]
        values[there, :HEAD_DIM] = far_ref[heads + h]
    values[:, HEAD_DIM:] = jnp.where(lane < 3, -1.0, 0.0).astype(BF16)
    lane = lane[:block]
    later = []
    parts = [slice(j * span, (j + 1) * span) for j in range(rows // span)]
    for step in range(rows // block):
        here = slice(step * block, (step + 1) * block)
        query = held_ref[0, here]
        scores = [dot(query, keys[p], NT) + bias_ref[j * span // half] for j, p in enumerate(parts)]
        begun = first_ref[h, here]
        own_peak = begun[:, HEAD_DIM + 1 : HEAD_DIM + 2]
        peak = functools.reduce(jnp.maximum, [jnp.max(s, axis=-1, keepdims=True) for s in scores])
        peak = jnp.maximum(peak * scale, own_peak)
        drop = jnp.exp2(own_peak - peak)
        mixed = begun * drop
        for p, one_scores in zip(parts, scores):
            raised = jnp.exp2(one_scores * scale - peak).astype(BF16)
            kept[here, p] = raised
            mixed = mixed + dot(raised, values[p])
        inverse = -1.0 / mixed[:, HEAD_DIM : HEAD_DIM + 1]
        grad = all_grads[here, head]
        attended = (mixed[:, :HEAD_DIM] * inverse).astype(BF16)
        out_ref[here, head] = attended
        dots = jnp.sum(grad.astype(F32) * attended.astype(F32), axis=-1, keepdims=True)
        rest_ref[h, here] = jnp.where(lane == 0, inverse * drop, dots)
        later.append((here, query, grad, dots, inverse))
    for step, (here, query, grad, dots, inverse) in enumerate(later):
        part_ref[here, head] = back_block(
            step, parts, [kept[here, p] for p in parts], query, grad, with_dots(grad, dots, lane), inverse, keys, values,
            dk_sum, dv_sum,
        )
    for out, first in ((low_ref, 0), (high_ref, half)):
        out[h] = (dk_sum[:, first : first + half].T * factor).astype(BF16)
        out[heads + h] = dv_sum[:, first : first + half].T.astype(BF16)


def back_kernel(heads, block, span, *refs):
    helds, refs = refs[:heads], refs[heads:]
    raw_ref, raised_ref, part_ref, rest_ref, all_grads, gain_ref = refs[:6]
    gq_ref, dk_ref, dv_ref = refs[6:9]
    rows = raw_ref.shape[1]
    lane = lax.broadcasted_iota(jnp.int32, (rows, HEAD_DIM), 1)
    parts = [slice(j * span, (j + 1) * span) for j in range(rows // span)]
    for h, held_ref in enumerate(helds):
        head = slice(h * HEAD_DIM, (h + 1) * HEAD_DIM)
        values, dk_sum, dv_sum = (pair.at[h % 2] for pair in refs[9:])
        values[:, :HEAD_DIM] = held_ref[2]
        values[:, HEAD_DIM:] = jnp.where(lane < 3, -1.0, 0.0).astype(BF16)
        for step in range(rows // block):
            here = slice(step * block, (step + 1) * block)
            rest = rest_ref[h, here]
            grad = all_grads[here, head]
            grad_wide = with_dots(grad, rest[:, 1:2], lane[:block])
            total = part_ref[here, head] + back_block(
                step, parts, [raised_ref[h, here, p] for p in parts], held_ref[0, here], grad,
                grad_wide, rest[:, :1], held_ref.at[1], values, dk_sum, dv_sum,
            )
            gq_ref[here, head] = norm_back(raw_ref[h, here], gain_ref[0:1], total)
        dk_ref[:, head] = dk_sum[...].T * HEAD_DIM**-0.5
        dv_ref[:, head] = dv_sum[...].T


def norm_back(raw, gain, grad):
    inverse_rms = lax.rsqrt(jnp.mean(raw * raw, axis=-1, keepdims=True) + EPSILON)
    weighted = grad * gain
    unit = raw * inverse_rms
    inner = jnp.mean(unit * weighted, axis=-1, keepdims=True)
    return (inverse_rms * (weighted - unit * inner)).astype(BF16)


def far_attention(bias, helds, far, first, out_grad, block=256, span=512):
    heads, rows = len(helds), helds[0].shape[1]
    width = heads * HEAD_DIM
    return on_chip(
        functools.partial(far_kernel, heads, block, span),
        [(bias, pltpu.SMEM), *helds, *far, first, out_grad],
        [((rows, width), BF16), ((rows, width), F32), ((heads, rows, HEAD_DIM), F32)]
        + [((2 * heads, rows // 2, HEAD_DIM), BF16)] * 2,
        [pltpu.VMEM((2, rows, HEAD_DIM), BF16), pltpu.VMEM((2, rows, 2 * HEAD_DIM), BF16)]
        + [pltpu.VMEM((2, HEAD_DIM, rows), F32)] * 2
        + [pltpu.VMEM((2, rows, rows), BF16)],
        us=15,
        name="far_attention",
    )


def back_attention(helds, raw, raised, part, rest, out_grad, gain, block=512, span=512):
    heads, rows = len(helds), helds[0].shape[1]
    width = heads * HEAD_DIM
    return on_chip(
        functools.partial(back_kernel, heads, block, span),
        [*helds, raw, raised, part, rest, out_grad, gain],
        [((rows, width), BF16)] + [((rows, width), F32)] * 2,
        [pltpu.VMEM((2, rows, 2 * HEAD_DIM), BF16)] + [pltpu.VMEM((2, HEAD_DIM, rows), F32)] * 2,
        us=13,
        name="back_attention",
    )


def split_rows(count, place_ref, straight, g, pieces, mine_ref, theirs_ref):
    chunk = straight.shape[0] // count
    for i in range(count):
        there = pl.ds(pl.multiple_of(place_ref[FIRST + i] * chunk, chunk), chunk)
        g[i * chunk : (i + 1) * chunk] = straight[there]
    blocks, rows, _ = mine_ref.shape
    low = place_ref[2] == 0
    for b in range(blocks):
        columns = slice(2 * b * rows, 2 * (b + 1) * rows)
        x = jnp.concatenate([piece[:, columns] for piece in pieces], 0)
        product = dot(x, g[...], TN).astype(BF16)
        mine_ref[b] = jnp.where(low, product[:rows], product[rows:])
        theirs_ref[b] = jnp.where(low, product[rows:], product[:rows])


def query_kernel(count, place_ref, gq_ref, *refs):
    mine_ref, theirs_ref, g = refs[-3:]
    split_rows(count, place_ref, gq_ref, g, refs[:-3], mine_ref, theirs_ref)


def key_value_kernel(
    count, heads, place_ref, dk_ref, dv_ref, same_ref, cross_ref, raw_ref, gain_ref, after_ref, *refs
):
    mine_ref, theirs_ref, straight, g = refs[-4:]
    half = dk_ref.shape[0] // 2
    for i, came in enumerate((same_ref, cross_ref)):
        mine = place_ref[3] if i == 0 else 1 - place_ref[3]
        rows = pl.ds(pl.multiple_of(mine * half, half), half)
        for h in range(heads):
            head = slice(h * HEAD_DIM, (h + 1) * HEAD_DIM)
            there = slice((heads + h) * HEAD_DIM, (heads + h + 1) * HEAD_DIM)
            dk = dk_ref[rows, head] + came[h].astype(F32)
            dv = dv_ref[rows, head] + came[heads + h].astype(F32)
            straight[rows, head] = norm_back(raw_ref[heads + h, rows], gain_ref[1:2], dk)
            straight[rows, there] = dv.astype(BF16)
    split_rows(count, place_ref, straight, g, refs[:-4], mine_ref, theirs_ref)


def weight_rows(kernel, groups, place, ins, total, width, held, us, name):
    pieces = [piece for group in groups for piece in group]
    out = ((8, pieces[0].shape[1] // 16, width), BF16)
    return on_chip(
        kernel,
        [(place, pltpu.SMEM), *ins, *pieces],
        [out, out],
        [pltpu.VMEM((total, width), BF16)] * held,
        us=us,
        name=name,
    )


def pair_kernel(place_ref, mine_q, came_q, mine_kv, came_kv, *outs):
    zh, x = place_ref[0], place_ref[1]
    rows = mine_q.shape[1] // 2
    along_x, (stay, leave) = outs[:4], outs[4:]
    at = 0
    for mine, came in ((mine_q, came_q), (mine_kv, came_kv)):
        columns = slice(at, at + mine.shape[2])
        at += mine.shape[2]
        for dx in range(4):
            for dz in range(2):
                b = ((zh + dz) % 2) * 4 + (x + dx) % 4
                both = (mine[b].astype(F32) + came[b].astype(F32)).astype(BF16)
                along_x[dx][dz, :, columns] = both[:rows]
                (leave if dz else stay)[dx, :, columns] = both[rows:]


def after_x_kernel(a_ref, b_ref, c_ref, d_ref, after_ref, keep_ref, send_ref):
    for i, out in enumerate((keep_ref, send_ref)):
        summed = a_ref[i].astype(F32) + b_ref[i].astype(F32)
        summed = summed + c_ref[i].astype(F32) + d_ref[i].astype(F32)
        out[...] = summed.astype(out.dtype)


def after_z_kernel(stay_ref, came_ref, *outs):
    for dx, out in enumerate(outs):
        out[...] = (stay_ref[dx].astype(F32) + came_ref[dx].astype(F32)).astype(out.dtype)


def last_kernel(keep_x, came_x, keep_z, a_ref, b_ref, c_ref, out):
    rows = keep_x.shape[0]
    top = keep_x[...] + came_x[...].astype(F32)
    bottom = keep_z[...] + a_ref[...].astype(F32)
    bottom = bottom + b_ref[...].astype(F32) + c_ref[...].astype(F32)
    width = out.shape[2]
    for kind in range(3):
        columns = slice(kind * width, (kind + 1) * width)
        out[kind, :rows] = top[:, columns]
        out[kind, rows:] = bottom[:, columns]


def halves_kernel(first_ref, last_ref, first_half, last_half):
    cut = first_half.shape[0]
    first_half[...] = first_ref[:cut]
    last_half[...] = last_ref[cut:]


def per_device(hidden, qkv_weight, norm_gain, out_grad):
    depth, kinds, local = qkv_weight.shape
    heads = local // HEAD_DIM
    chunk = hidden.shape[0]
    total = chunk * lax.axis_size("tensor")
    half = total // 2
    frame = lax.axis_index("frame").astype(jnp.int32)
    frames = lax.axis_size("frame")
    tensor = lax.axis_index("tensor").astype(jnp.int32)
    zh, x, core = frame // 8, (frame // 2) % 4, frame % 2
    y, zl = tensor // 2, tensor % 2
    def at(dy, dz):
        return ((y + dy) % 4) * 2 + (zl + dz) % 2

    weight = qkv_weight.transpose(1, 0, 2)

    send = lambda value, dy, dz: lax.ppermute(value, "tensor", tensor_pairs(dy, dz))
    cut = chunk // 2
    below = send(hidden, 1, 0)
    above = send(hidden, -1, 0)
    side = send(hidden, 0, 1)
    far = send(above, -1, 0)
    side_above = send(above, 0, 1)
    side_below = send(side, 1, 0)
    first_half, last_half = on_chip(
        halves_kernel, [side_above, far], [((cut, depth), BF16)] * 2, name="halves"
    )
    side_far = (send(first_half, -1, 0), send(last_half, 0, 1))
    groups = [(hidden,), (below,), (above,), (side,), (far,), (side_below,), (side_above,), side_far]
    moves = [(0, 0), (-1, 0), (1, 0), (0, 1), (2, 0), (-1, 1), (1, 1), (2, 1)]
    mine = y // 2
    place = jnp.stack([zh, x, core, mine] + [at(*move) for move in moves])

    def proj(first, last, before, extra, us):
        return project(
            place, first, groups[first:last], weight, norm_gain, heads, total, before, extra, us
        )

    move = lambda value, pairs: lax.ppermute(value, ("frame", "tensor"), pairs)
    state = proj(0, 4, None, 0, 6)
    state = proj(4, 7, state, 0, 5)
    raw, *held, same, cross = proj(7, 8, state, 2, 2)
    far = (move(same, half_pairs(1)), move(cross, half_pairs(-1)))
    turn = 2 * mine - 1
    seen = lambda f: jnp.where((f >= 0) & (f < frames), 0.0, -1e30).astype(F32)
    bias = jnp.stack([seen(frame - turn), seen(frame + turn)])

    raised, first = own_attention(held)
    attended, part, rest, low, high = far_attention(bias, held, far, first, out_grad)
    gq, dk, dv = back_attention(held, raw, raised, part, rest, out_grad, norm_gain)
    same = move(low, [pair[::-1] for pair in half_pairs(1)])
    cross = move(high, [pair[::-1] for pair in half_pairs(-1)])
    count = len(groups)
    swap = lambda value: lax.ppermute(value, "frame", frame_pairs(0, 0, 1))
    mine_q, theirs_q = weight_rows(
        functools.partial(query_kernel, count), groups, place, [gq], total, local, 1, 5, "query"
    )
    mine_kv, theirs_kv = weight_rows(
        functools.partial(key_value_kernel, count, heads),
        groups,
        place,
        [dk, dv, same, cross, raw, norm_gain, (mine_q, pl.ANY)],
        total,
        2 * local,
        2,
        8,
        "key_value",
    )
    rows = mine_q.shape[1] // 2
    wide = kinds * local
    piece = ((2, rows, wide), BF16)
    line = ((4, rows, wide), BF16)
    *along_x, stay, leave = on_chip(
        pair_kernel,
        [(place, pltpu.SMEM), mine_q, swap(theirs_q), mine_kv, swap(theirs_kv)],
        [piece] * 4 + [line] * 2,
        name="pair",
    )
    shift = lambda value, dx, dz: lax.ppermute(value, "frame", frame_pairs(dx, dz))
    came = shift(leave, 0, 1)
    moved = [shift(along_x[dx], dx, 0) for dx in (2, 1, 3)]
    one = (rows, wide)
    keep_z, *send_z = on_chip(
        after_z_kernel, [stay, came], [(one, F32)] + [(one, BF16)] * 3, name="after_z"
    )
    came_z = [shift(send_z[dx - 1], dx, 0) for dx in (2, 1, 3)]
    keep_x, send_x = on_chip(
        after_x_kernel, [along_x[0], *moved, (keep_z, pl.ANY)], [(one, F32), (one, BF16)], name="after_x"
    )
    came_x = shift(send_x, 0, 1)
    (weight_grad,) = on_chip(
        last_kernel,
        [keep_x, came_x, keep_z, *came_z],
        [((kinds, 2 * rows, local), F32)],
        name="last",
    )
    return (attended, weight_grad.transpose(1, 0, 2))


def solution(mesh):
    placed = (P(("frame", "tensor"), None), P(None, None, "tensor"), P(), P("frame", "tensor"))
    return jax.shard_map(
        per_device,
        mesh=mesh,
        in_specs=placed,
        out_specs=(P("frame", "tensor"), P("frame", None, "tensor")),
        check_vma=False,
    )
```
